32 devices in a mesh: rep: 8 (over y, x, core), fsdp: 4 (over z).
Axes of the slice: x: 2, y: 2, z: 4, core: 2. Of those that a mesh axis runs over, the one named last changes fastest.
Arguments:
- tokens: bfloat16 [8, 1024, 4096], P('rep', 'fsdp'), may hold values from -90 to 90
- cotangent: bfloat16 [8, 1024, 2048], P('rep', 'fsdp'), may hold values from -6 to 6
- w_slow: bfloat16 [8, 4096, 2048], P('rep', 'fsdp'), may hold values from -6 to 6
- drift: bfloat16 [8, 4096, 2048], P('rep', 'fsdp'), may hold values from -4 to 4
- momentum: bfloat16 [8, 4096, 2048], P('rep', 'fsdp'), may hold values from -4 to 4
- partner: int32 [8], replicated, may hold values from 0 to 7, as said below
Outputs:
- momentum_new: bfloat16 [8, 4096, 2048], P('rep', 'fsdp')
- weights_new: bfloat16 [8, 4096, 2048], P('rep', 'fsdp')
The draws below stay inside these ranges and needn't reach their ends.
Inputs may be any that keep to these rules, and one draw needn't show every extreme that they name: partner[partner[r]] == r and partner[r] != r for every replica r.
All inputs are finite; a program needn't handle non-finite values.
Results may differ from the reference program's by a relative error of at most 0.013.
Values may be sent and summed in bfloat16 or wider, within the bound.
A program may use at most 128 MiB of HBM per device.

```python
import math
import jax
import jax.numpy as jnp
from jax import lax

D = 4096
DO = 2048
TOK_DEV = 256
TOK_REP = 1024
REPLICAS = 8
N_REP = 8
N_FSDP = 4


def draw_tokens(key, part):
    key = jax.random.fold_in(key, 11)
    first, second = jax.random.split(key)
    column = jnp.arange(D, dtype=jnp.float32) / D
    rising = jnp.exp(math.log(10.0) * column)
    base = jax.random.truncated_normal(first, -6.0, 6.0, (REPLICAS, TOK_REP, D), jnp.float32)
    factor = jnp.exp(jax.random.uniform(second, (D,), jnp.float32, math.log(0.7), math.log(1.4)))
    return (base * rising * factor).astype(jnp.bfloat16)


def draw_partner(key, part):
    key = jax.random.fold_in(key, 23)
    order = jax.random.permutation(key, REPLICAS).astype(jnp.int32)
    flipped = order.reshape(REPLICAS // 2, 2)[:, ::-1].reshape(REPLICAS)
    return jnp.zeros((REPLICAS,), jnp.int32).at[order].set(flipped)


def block_levels(rng, shape, cuts, low, high):
    gain, own = 1.0, jax.random.fold_in(rng, 6)
    for axis_at, blocks in cuts:
        steps = jnp.exp(jax.random.uniform(jax.random.fold_in(own, axis_at), (blocks,), jnp.float32, low / len(cuts), high / len(cuts)))
        gain = gain * jnp.repeat(steps, shape[axis_at] // blocks).reshape([-1 if axis == axis_at else 1 for axis in range(len(shape))])
    return gain


def noise(key, shape, deviation, limit, cuts=(), held_as=jnp.bfloat16):
    loudness = block_levels(key, shape, cuts, -0.22, 0.18) if cuts else 1.0
    drawn = jax.random.normal(key, shape, jnp.float32) * deviation * loudness
    return jnp.minimum(jnp.maximum(drawn, -limit), limit).astype(held_as)


def setup_inputs(seed: int = 0) -> dict:
    arg_keys = jax.random.split(jax.random.key(seed), 7)
    return {
        "tokens": draw_tokens(jax.random.fold_in(arg_keys[6], 71), 0),
        "cotangent": noise(arg_keys[1], (REPLICAS, TOK_REP, DO), 1.0, 6.0, ((0, 8), (1, 4))),
        "w_slow": noise(arg_keys[2], (REPLICAS, D, DO), 1.0, 6.0, ((0, 8), (1, 4))),
        "drift": noise(arg_keys[3], (REPLICAS, D, DO), 0.5, 4.0, ((0, 8), (1, 4))),
        "momentum": noise(arg_keys[4], (REPLICAS, D, DO), 0.5, 4.0, ((0, 8), (1, 4))),
        "partner": draw_partner(jax.random.fold_in(arg_keys[6], 71), 0),
    }


def one_replica(index, tokens, cotangent, w_slow, drift, momentum, partner):
    token_blocks = tokens[index].astype(jnp.float32).reshape(N_FSDP, TOK_DEV, D)
    grad_blocks = cotangent[index].astype(jnp.float32).reshape(N_FSDP, TOK_DEV, DO)

    def add_block(total, pair):
        block_x, block_g = pair
        partial_sum = jnp.dot(block_x.T, block_g, precision=lax.Precision.HIGHEST)
        rounded = lax.optimization_barrier(partial_sum.astype(jnp.bfloat16))
        return (total + rounded.astype(jnp.float32), None)
    grad, unused = lax.scan(add_block, jnp.zeros((D, DO), jnp.float32), (token_blocks, grad_blocks))
    scale = jnp.sqrt(jnp.mean(grad * grad) + 1e-06)
    mate = partner[index]
    partner_mix = (0.5 * (0.7 * drift[mate].astype(jnp.float32) - 0.3 * w_slow[mate].astype(jnp.float32))).astype(jnp.bfloat16)
    own_slow = w_slow[index].astype(jnp.float32)
    moment = 0.5 * momentum[index].astype(jnp.float32) + 0.35 * drift[index].astype(jnp.float32) + 0.15 * own_slow + partner_mix.astype(jnp.float32)
    weights = own_slow - moment - 0.5 * grad / scale
    return (moment.astype(jnp.bfloat16), weights.astype(jnp.bfloat16))

def reference(tokens, cotangent, w_slow, drift, momentum, partner):

    def step(index):
        return one_replica(index, tokens, cotangent, w_slow, drift, momentum, partner)
    momentum_new, weights_new = lax.map(step, jnp.arange(N_REP, dtype=jnp.int32))
    return (momentum_new, weights_new)
```

```python
import functools

import jax
import jax.numpy as jnp
from jax import lax
from jax.experimental import pallas as pl
from jax.experimental.pallas import tpu as pltpu
from jax.sharding import PartitionSpec as P

MESH = pl.DeviceIdType.MESH
CHUNKS = 4
F32 = jnp.float32
BF16 = jnp.bfloat16


def kernel(reps, n, *refs):
    C = CHUNKS
    (tok, cot, slow, drift, mom, partner, mom_out, w_out) = refs[:8]
    (wv, dv, mv, base, grad, tokv, cotv, mixsrc, mixin, squares, acc) = refs[8:19]
    owned = refs[19 : 19 + C]
    (ld, tsend, trecv, crecv, crsend, clsend, asend, arecv, bsend, brecv, qsend, qrecv, out_sem) = refs[19 + C :]
    me = lax.axis_index("rep")
    z = lax.axis_index("fsdp")
    rows = wv.shape[1]
    cw = wv.shape[2]
    rp = rows // reps
    cd = tokv.shape[2]

    def cols(c):
        return pl.ds(c * cw, cw)

    def load(kind, c):
        src, dst = ((slow, wv), (drift, dv), (mom, mv))[kind]
        return pltpu.make_async_copy(src.at[0, :, cols(c)], dst.at[c], ld.at[kind, c])

    def load_cot(q):
        return pltpu.make_async_copy(cot.at[0, :, cols(q)], cotv.at[q, z], ld.at[3, q])

    def tok_cols(k):
        return pl.ds(pl.multiple_of(k * cd, 128), cd)

    load_tok = pltpu.make_async_copy(tok.at[0, :, tok_cols(z)], tokv.at[z], ld.at[4, 0])

    for c in range(C):
        load(0, c).start()
        load(1, c).start()

    barrier = pltpu.get_barrier_semaphore()
    for d in range(1, n):
        pl.semaphore_signal(barrier, inc=1, device_id=(me, lax.rem(z + d, n)), device_id_type=MESH)

    def greet(d, _):
        pl.semaphore_signal(barrier, inc=1, device_id=(lax.rem(me + d, reps), z), device_id_type=MESH)
        return 0

    lax.fori_loop(1, reps, greet, 0)
    for q in range(C):
        load_cot(q).start()
    load_tok.start()
    for c in range(C):
        load(2, c).start()
    pl.semaphore_wait(barrier, reps - 1 + n - 1)

    def right_copy(q, s, src):
        return pltpu.make_async_remote_copy(
            src_ref=src, dst_ref=cotv.at[q, s], send_sem=crsend.at[q, s], recv_sem=crecv.at[q, s],
            device_id=(me, lax.min(z + 1, n - 1)), device_id_type=MESH)

    def left_copy(q, s, src):
        return pltpu.make_async_remote_copy(
            src_ref=src, dst_ref=cotv.at[q, s], send_sem=clsend.at[q, s], recv_sem=crecv.at[q, s],
            device_id=(me, lax.max(z - 1, 0)), device_id_type=MESH)

    for q in range(C):
        @pl.when(z + 1 < n)
        def _():
            right_copy(q, z, cot.at[0, :, cols(q)]).start()

        @pl.when(z > 0)
        def _():
            left_copy(q, z, cot.at[0, :, cols(q)]).start()

    def tok_copy(d):
        k = lax.rem(z + d, n)
        return pltpu.make_async_remote_copy(
            src_ref=tok.at[0, :, tok_cols(k)], dst_ref=tokv.at[z], send_sem=tsend.at[d], recv_sem=trecv.at[d],
            device_id=(me, k), device_id_type=MESH)

    for d in range(1, n):
        tok_copy(d).start()

    def first_leg(c, d):
        j = lax.rem(me + d, reps)
        return pltpu.make_async_remote_copy(
            src_ref=mixsrc.at[c, j], dst_ref=owned[c].at[me], send_sem=asend.at[c, d], recv_sem=arecv.at[c, d],
            device_id=(j, z), device_id_type=MESH)

    def first_leg_in(c, d):
        s = lax.rem(me + reps - d, reps)
        return pltpu.make_async_remote_copy(
            src_ref=mixsrc.at[c, s], dst_ref=owned[c].at[s], send_sem=asend.at[c, d], recv_sem=arecv.at[c, d],
            device_id=(s, z), device_id_type=MESH)

    def second_leg(c, d):
        j = lax.rem(me + d, reps)
        return pltpu.make_async_remote_copy(
            src_ref=mixsrc.at[c, j], dst_ref=mixin.at[c, me], send_sem=bsend.at[c, d], recv_sem=brecv.at[c, d],
            device_id=(j, z), device_id_type=MESH)

    def second_leg_in(c, d):
        s = lax.rem(me + reps - d, reps)
        return pltpu.make_async_remote_copy(
            src_ref=mixsrc.at[c, s], dst_ref=mixin.at[c, s], send_sem=bsend.at[c, d], recv_sem=brecv.at[c, d],
            device_id=(s, z), device_id_type=MESH)

    def block_rows(j):
        return pl.ds(pl.multiple_of(j * rp, rp), rp)

    def mix_block(c, j):
        part = block_rows(j)
        return (0.5 * (0.7 * dv[c, part, :].astype(F32) - 0.3 * wv[c, part, :].astype(F32))).astype(BF16)

    for c in range(C):
        load(0, c).wait()
        load(1, c).wait()

        def send_block(d, _):
            j = lax.rem(me + d, reps)
            mixsrc[c, j] = mix_block(c, j)
            first_leg(c, d).start()
            return 0

        lax.fori_loop(1, reps, send_block, 0)
        owned[c][me] = mix_block(c, me)

    def turn_round(c):
        def arrived(d, _):
            first_leg_in(c, d).wait_recv()
            first_leg(c, d).wait_send()
            return 0

        lax.fori_loop(1, reps, arrived, 0)

        def send_back(d, _):
            j = lax.rem(me + d, reps)
            mixsrc[c, j] = owned[c][partner[j]]
            second_leg(c, d).start()
            return 0

        lax.fori_loop(1, reps, send_back, 0)
        mixin[c, me] = owned[c][partner[me]]

    def finish_momentum(c):
        load(2, c).wait()

        def arrived(d, _):
            second_leg_in(c, d).wait_recv()
            return 0

        lax.fori_loop(1, reps, arrived, 0)

        def block(j, _):
            part = block_rows(j)
            own = wv[c, part, :].astype(F32)
            moment = (0.5 * mv[c, part, :].astype(F32) + 0.35 * dv[c, part, :].astype(F32) + 0.15 * own
                      + mixin[c, j].astype(F32))
            mv[c, part, :] = moment.astype(BF16)
            base[c, part, :] = own - moment
            return 0

        lax.fori_loop(0, reps, block, 0)
        pltpu.make_async_copy(mv.at[c], mom_out.at[0, :, cols(c)], out_sem.at[0, c]).start()

    tile = 256

    def product(q, s, first):
        def block(i, _):
            part = pl.ds(pl.multiple_of(i * tile, tile), tile)
            term = lax.dot_general(
                tokv[s, :, part], cotv[q, s], (((0,), (0,)), ((), ())), preferred_element_type=F32
            ).astype(BF16).astype(F32)
            if first:
                grad[q, part, :] = term
            else:
                grad[q, part, :] += term
            return 0

        lax.fori_loop(0, rows // tile, block, 0)

    def add_squares(q):
        def block(i, _):
            g = grad[q, pl.ds(pl.multiple_of(i * 64, 64), 64), :]
            acc[...] += jnp.sum((g * g).reshape(8, 8, cw), axis=0)
            return 0

        lax.fori_loop(0, rows // 64, block, 0)

    def arrive(h, q):
        @pl.when(z - h >= 0)
        def _():
            s = lax.max(z - h, 0)
            right_copy(q, s, cotv.at[q, s]).wait_recv()

            @pl.when(z + 1 < n)
            def _():
                right_copy(q, s, cotv.at[q, s]).start()

        @pl.when(z + h < n)
        def _():
            s = lax.min(z + h, n - 1)
            left_copy(q, s, cotv.at[q, s]).wait_recv()

            @pl.when(z > 0)
            def _():
                left_copy(q, s, cotv.at[q, s]).start()

    def multiply(h, q):
        @pl.when(z - h >= 0)
        def _():
            s = lax.max(z - h, 0)
            if q == 0:
                tok_in(s, h).wait_recv()
            product(q, s, False)

        @pl.when(z + h < n)
        def _():
            s = lax.min(z + h, n - 1)
            if q == 0:
                tok_in(s, n - h).wait_recv()
            product(q, s, False)

        @pl.when(lax.max(z, n - 1 - z) == h)
        def _():
            add_squares(q)

    def tok_in(s, d):
        return pltpu.make_async_remote_copy(
            src_ref=tokv.at[s], dst_ref=tokv.at[s], send_sem=tsend.at[d], recv_sem=trecv.at[d],
            device_id=(me, s), device_id_type=MESH)

    acc[...] = jnp.zeros_like(acc)
    load_tok.wait()
    for q in range(C):
        load_cot(q).wait()
        product(q, z, True)
    for h in range(1, n):
        for q in range(C):
            if h == n - 1:
                finish_momentum(q)
            arrive(h, q)
            if h == 1:
                turn_round(q)
            if h > 1:
                multiply(h - 1, q)
            if h == n - 1:
                multiply(h, q)

    part_sum = acc[:, 0:128]
    for k in range(1, cw // 128):
        part_sum = part_sum + acc[:, k * 128 : (k + 1) * 128]
    squares[z] = part_sum

    def squares_copy(d):
        k = lax.rem(z + d, n)
        return pltpu.make_async_remote_copy(
            src_ref=squares.at[z], dst_ref=squares.at[z], send_sem=qsend.at[d], recv_sem=qrecv.at[d],
            device_id=(me, k), device_id_type=MESH)

    for d in range(1, n):
        squares_copy(d).start()
    for d in range(1, n):
        s = lax.rem(z + n - d, n)
        pltpu.make_async_remote_copy(
            src_ref=squares.at[s], dst_ref=squares.at[s], send_sem=qsend.at[d], recv_sem=qrecv.at[d],
            device_id=(me, s), device_id_type=MESH).wait_recv()
    total = jnp.sum(jnp.sum(squares[...], axis=0), axis=(0, 1), keepdims=True)
    factor = 0.5 / jnp.sqrt(total / (rows * n * C * cw) + 1e-06)

    for q in range(C):
        def block(i, _):
            part = pl.ds(pl.multiple_of(i * 64, 64), 64)
            wv[q, part, :] = (base[q, part, :] - grad[q, part, :] * factor).astype(BF16)
            return 0

        lax.fori_loop(0, rows // 64, block, 0)
        pltpu.make_async_copy(wv.at[q], w_out.at[0, :, cols(q)], out_sem.at[1, q]).start()

    for d in range(1, n):
        tok_copy(d).wait_send()
        squares_copy(d).wait_send()
    for q in range(C):
        for h in range(0, n):
            @pl.when((z - h >= 0) & (z + 1 < n))
            def _():
                s = lax.max(z - h, 0)
                right_copy(q, s, cotv.at[q, s]).wait_send()

            @pl.when((z + h < n) & (z > 0))
            def _():
                s = lax.min(z + h, n - 1)
                left_copy(q, s, cotv.at[q, s]).wait_send()

        def sent(d, _):
            second_leg(q, d).wait_send()
            return 0

        lax.fori_loop(1, reps, sent, 0)
    for q in range(C):
        pltpu.make_async_copy(mv.at[q], mom_out.at[0, :, cols(q)], out_sem.at[0, q]).wait()
        pltpu.make_async_copy(wv.at[q], w_out.at[0, :, cols(q)], out_sem.at[1, q]).wait()


def on_device(reps, n, tokens, cotangent, w_slow, drift, momentum, partner):
    C = CHUNKS
    _, toks, d_in = tokens.shape
    _, rows, d_out = w_slow.shape
    cw, rp, cd = d_out // C, rows // reps, d_in // n
    hbm = pl.BlockSpec(memory_space=pl.ANY)
    dma = pltpu.SemaphoreType.DMA
    scratch = [
        pltpu.VMEM((C, rows, cw), BF16),
        pltpu.VMEM((C, rows, cw), BF16),
        pltpu.VMEM((C, rows, cw), BF16),
        pltpu.VMEM((C, rows, cw), F32),
        pltpu.VMEM((C, rows, cw), F32),
        pltpu.VMEM((n, toks, cd), BF16),
        pltpu.VMEM((C, n, toks, cw), BF16),
        pltpu.VMEM((C, reps, rp, cw), BF16),
        pltpu.VMEM((C, reps, rp, cw), BF16),
        pltpu.VMEM((n, 8, 128), F32),
        pltpu.VMEM((8, cw), F32),
    ]
    scratch += [pltpu.VMEM((reps, rp, cw), BF16) for _ in range(C)]
    scratch += [
        dma((5, C)), dma((n,)), dma((n,)), dma((C, n)), dma((C, n)), dma((C, n)),
        dma((C, reps)), dma((C, reps)), dma((C, reps)), dma((C, reps)), dma((n,)), dma((n,)), dma((2, C)),
    ]
    return pl.pallas_call(
        functools.partial(kernel, reps, n),
        out_shape=(jax.ShapeDtypeStruct(momentum.shape, BF16), jax.ShapeDtypeStruct(w_slow.shape, BF16)),
        in_specs=[hbm] * 5 + [pl.BlockSpec(memory_space=pltpu.SMEM)],
        out_specs=(hbm, hbm),
        scratch_shapes=scratch,
        compiler_params=pltpu.CompilerParams(
            collective_id=0, has_side_effects=True, vmem_limit_bytes=56 * 1024 * 1024
        ),
        cost_estimate=pl.CostEstimate(
            flops=2 * n * toks * rows * d_out, bytes_accessed=5 * rows * d_out * 2, transcendentals=0
        ),
    )(tokens, cotangent, w_slow, drift, momentum, partner)


def solution(mesh):
    spec = P("rep", "fsdp", None)
    return jax.shard_map(
        functools.partial(on_device, mesh.shape["rep"], mesh.shape["fsdp"]),
        mesh=mesh,
        in_specs=(spec, spec, spec, spec, spec, P()),
        out_specs=(spec, spec),
        check_vma=False,
    )
```

```python
import functools

import jax
import jax.numpy as jnp
from jax import lax
from jax.experimental import pallas as pl
from jax.experimental.pallas import tpu as pltpu
from jax.sharding import PartitionSpec as P

MESH = pl.DeviceIdType.MESH
CHUNKS = 4
F32 = jnp.float32
BF16 = jnp.bfloat16


def kernel(reps, n, *refs):
    C = CHUNKS
    (tok, cot, slow, drift, mom, partner, mom_out, base, grad, factor_out) = refs[:10]
    (wv, dv, mv, tokv, cotv, mixsrc, mixin, squares, acc) = refs[10:19]
    owned = refs[19 : 19 + C]
    (ld, tsend, trecv, crecv, crsend, clsend, asend, arecv, bsend, brecv, qsend, qrecv) = refs[19 + C :]
    me = lax.axis_index("rep")
    z = lax.axis_index("fsdp")
    rows = wv.shape[1]
    cw = wv.shape[2]
    rp = rows // reps
    cd = tokv.shape[2]

    def cols(c):
        return pl.ds(c * cw, cw)

    def load(kind, c):
        src, dst = ((slow, wv), (drift, dv), (mom, mv))[kind]
        return pltpu.make_async_copy(src.at[0, :, cols(c)], dst.at[c], ld.at[kind, c])

    def load_cot(q):
        return pltpu.make_async_copy(cot.at[0, :, cols(q)], cotv.at[q, z], ld.at[3, q])

    def tok_cols(k):
        return pl.ds(pl.multiple_of(k * cd, 128), cd)

    load_tok = pltpu.make_async_copy(tok.at[0, :, tok_cols(z)], tokv.at[z], ld.at[4, 0])

    for c in range(C):
        load(0, c).start()
        load(1, c).start()

    barrier = pltpu.get_barrier_semaphore()
    for d in range(1, n):
        pl.semaphore_signal(barrier, inc=1, device_id=(me, lax.rem(z + d, n)), device_id_type=MESH)

    def greet(d, _):
        pl.semaphore_signal(barrier, inc=1, device_id=(lax.rem(me + d, reps), z), device_id_type=MESH)
        return 0

    lax.fori_loop(1, reps, greet, 0)
    for q in range(C):
        load_cot(q).start()
    load_tok.start()
    for c in range(C):
        load(2, c).start()
    pl.semaphore_wait(barrier, reps - 1 + n - 1)

    def right_copy(q, s, src):
        return pltpu.make_async_remote_copy(
            src_ref=src, dst_ref=cotv.at[q, s], send_sem=crsend.at[q, s], recv_sem=crecv.at[q, s],
            device_id=(me, lax.min(z + 1, n - 1)), device_id_type=MESH)

    def left_copy(q, s, src):
        return pltpu.make_async_remote_copy(
            src_ref=src, dst_ref=cotv.at[q, s], send_sem=clsend.at[q, s], recv_sem=crecv.at[q, s],
            device_id=(me, lax.max(z - 1, 0)), device_id_type=MESH)

    for q in range(C):
        @pl.when(z + 1 < n)
        def _():
            right_copy(q, z, cot.at[0, :, cols(q)]).start()

        @pl.when(z > 0)
        def _():
            left_copy(q, z, cot.at[0, :, cols(q)]).start()

    def tok_copy(d):
        k = lax.rem(z + d, n)
        return pltpu.make_async_remote_copy(
            src_ref=tok.at[0, :, tok_cols(k)], dst_ref=tokv.at[z], send_sem=tsend.at[d], recv_sem=trecv.at[d],
            device_id=(me, k), device_id_type=MESH)

    for d in range(1, n):
        tok_copy(d).start()

    def first_leg(c, d):
        j = lax.rem(me + d, reps)
        return pltpu.make_async_remote_copy(
            src_ref=mixsrc.at[c, j], dst_ref=owned[c].at[me], send_sem=asend.at[c, d], recv_sem=arecv.at[c, d],
            device_id=(j, z), device_id_type=MESH)

    def first_leg_in(c, d):
        s = lax.rem(me + reps - d, reps)
        return pltpu.make_async_remote_copy(
            src_ref=mixsrc.at[c, s], dst_ref=owned[c].at[s], send_sem=asend.at[c, d], recv_sem=arecv.at[c, d],
            device_id=(s, z), device_id_type=MESH)

    def second_leg(c, d):
        j = lax.rem(me + d, reps)
        return pltpu.make_async_remote_copy(
            src_ref=mixsrc.at[c, j], dst_ref=mixin.at[c, me], send_sem=bsend.at[c, d], recv_sem=brecv.at[c, d],
            device_id=(j, z), device_id_type=MESH)

    def second_leg_in(c, d):
        s = lax.rem(me + reps - d, reps)
        return pltpu.make_async_remote_copy(
            src_ref=mixsrc.at[c, s], dst_ref=mixin.at[c, s], send_sem=bsend.at[c, d], recv_sem=brecv.at[c, d],
            device_id=(s, z), device_id_type=MESH)

    def block_rows(j):
        return pl.ds(pl.multiple_of(j * rp, rp), rp)

    def mix_block(c, j):
        part = block_rows(j)
        return (0.5 * (0.7 * dv[c, part, :].astype(F32) - 0.3 * wv[c, part, :].astype(F32))).astype(BF16)

    for c in range(C):
        load(0, c).wait()
        load(1, c).wait()

        def send_block(d, _):
            j = lax.rem(me + d, reps)
            mixsrc[c, j] = mix_block(c, j)
            first_leg(c, d).start()
            return 0

        lax.fori_loop(1, reps, send_block, 0)
        owned[c][me] = mix_block(c, me)

    def turn_round(c):
        def arrived(d, _):
            first_leg_in(c, d).wait_recv()
            first_leg(c, d).wait_send()
            return 0

        lax.fori_loop(1, reps, arrived, 0)

        def send_back(d, _):
            j = lax.rem(me + d, reps)
            mixsrc[c, j] = owned[c][partner[j]]
            second_leg(c, d).start()
            return 0

        lax.fori_loop(1, reps, send_back, 0)
        mixin[c, me] = owned[c][partner[me]]

    def finish_momentum(c):
        load(2, c).wait()

        def arrived(d, _):
            second_leg_in(c, d).wait_recv()
            return 0

        lax.fori_loop(1, reps, arrived, 0)

        def block(j, _):
            part = block_rows(j)
            own = wv[c, part, :].astype(F32)
            moment = (0.5 * mv[c, part, :].astype(F32) + 0.35 * dv[c, part, :].astype(F32) + 0.15 * own
                      + mixin[c, j].astype(F32))
            mom_out[0, part, cols(c)] = moment.astype(BF16)
            base[0, part, cols(c)] = own - moment
            return 0

        lax.fori_loop(0, reps, block, 0)

    tile = 256

    def product(q, s, first):
        def block(i, _):
            part = pl.ds(pl.multiple_of(i * tile, tile), tile)
            term = lax.dot_general(
                tokv[s, :, part], cotv[q, s], (((0,), (0,)), ((), ())), preferred_element_type=F32
            ).astype(BF16).astype(F32)
            if first:
                grad[0, part, cols(q)] = term
            else:
                grad[0, part, cols(q)] += term
            return 0

        lax.fori_loop(0, rows // tile, block, 0)

    def add_squares(q):
        def block(i, _):
            g = grad[0, pl.ds(pl.multiple_of(i * 64, 64), 64), cols(q)]
            acc[...] += jnp.sum((g * g).reshape(8, 8, cw), axis=0)
            return 0

        lax.fori_loop(0, rows // 64, block, 0)

    def arrive(h, q):
        @pl.when(z - h >= 0)
        def _():
            s = lax.max(z - h, 0)
            right_copy(q, s, cotv.at[q, s]).wait_recv()

            @pl.when(z + 1 < n)
            def _():
                right_copy(q, s, cotv.at[q, s]).start()

        @pl.when(z + h < n)
        def _():
            s = lax.min(z + h, n - 1)
            left_copy(q, s, cotv.at[q, s]).wait_recv()

            @pl.when(z > 0)
            def _():
                left_copy(q, s, cotv.at[q, s]).start()

    def multiply(h, q):
        @pl.when(z - h >= 0)
        def _():
            s = lax.max(z - h, 0)
            if q == 0:
                tok_in(s, h).wait_recv()
            product(q, s, False)

        @pl.when(z + h < n)
        def _():
            s = lax.min(z + h, n - 1)
            if q == 0:
                tok_in(s, n - h).wait_recv()
            product(q, s, False)

        @pl.when(lax.max(z, n - 1 - z) == h)
        def _():
            add_squares(q)

    def tok_in(s, d):
        return pltpu.make_async_remote_copy(
            src_ref=tokv.at[s], dst_ref=tokv.at[s], send_sem=tsend.at[d], recv_sem=trecv.at[d],
            device_id=(me, s), device_id_type=MESH)

    acc[...] = jnp.zeros_like(acc)
    load_tok.wait()
    for q in range(C):
        load_cot(q).wait()
        product(q, z, True)
    for h in range(1, n):
        for q in range(C):
            if h == n - 1:
                finish_momentum(q)
            arrive(h, q)
            if h == 1:
                turn_round(q)
            if h > 1:
                multiply(h - 1, q)
            if h == n - 1:
                multiply(h, q)

    part_sum = acc[:, 0:128]
    for k in range(1, cw // 128):
        part_sum = part_sum + acc[:, k * 128 : (k + 1) * 128]
    squares[z] = part_sum

    def squares_copy(d):
        k = lax.rem(z + d, n)
        return pltpu.make_async_remote_copy(
            src_ref=squares.at[z], dst_ref=squares.at[z], send_sem=qsend.at[d], recv_sem=qrecv.at[d],
            device_id=(me, k), device_id_type=MESH)

    for d in range(1, n):
        squares_copy(d).start()
    for d in range(1, n):
        s = lax.rem(z + n - d, n)
        pltpu.make_async_remote_copy(
            src_ref=squares.at[s], dst_ref=squares.at[s], send_sem=qsend.at[d], recv_sem=qrecv.at[d],
            device_id=(me, s), device_id_type=MESH).wait_recv()
    total = jnp.sum(jnp.sum(squares[...], axis=0), axis=(0, 1), keepdims=True)
    factor = 0.5 / jnp.sqrt(total / (rows * n * C * cw) + 1e-06)
    factor_out[...] = jnp.broadcast_to(factor[None], factor_out.shape)

    for d in range(1, n):
        tok_copy(d).wait_send()
        squares_copy(d).wait_send()
    for q in range(C):
        for h in range(0, n):
            @pl.when((z - h >= 0) & (z + 1 < n))
            def _():
                s = lax.max(z - h, 0)
                right_copy(q, s, cotv.at[q, s]).wait_send()

            @pl.when((z + h < n) & (z > 0))
            def _():
                s = lax.min(z + h, n - 1)
                left_copy(q, s, cotv.at[q, s]).wait_send()

        def sent(d, _):
            second_leg(q, d).wait_send()
            return 0

        lax.fori_loop(1, reps, sent, 0)


def on_device(reps, n, tokens, cotangent, w_slow, drift, momentum, partner):
    C = CHUNKS
    _, toks, d_in = tokens.shape
    _, rows, d_out = w_slow.shape
    cw, rp, cd = d_out // C, rows // reps, d_in // n
    hbm = pl.BlockSpec(memory_space=pl.ANY)
    dma = pltpu.SemaphoreType.DMA
    scratch = [
        pltpu.VMEM((C, rows, cw), BF16),
        pltpu.VMEM((C, rows, cw), BF16),
        pltpu.VMEM((C, rows, cw), BF16),
        pltpu.VMEM((n, toks, cd), BF16),
        pltpu.VMEM((C, n, toks, cw), BF16),
        pltpu.VMEM((C, reps, rp, cw), BF16),
        pltpu.VMEM((C, reps, rp, cw), BF16),
        pltpu.VMEM((n, 8, 128), F32),
        pltpu.VMEM((8, cw), F32),
    ]
    scratch += [pltpu.VMEM((reps, rp, cw), BF16) for _ in range(C)]
    scratch += [
        dma((5, C)), dma((n,)), dma((n,)), dma((C, n)), dma((C, n)), dma((C, n)),
        dma((C, reps)), dma((C, reps)), dma((C, reps)), dma((C, reps)), dma((n,)), dma((n,)),
    ]
    moment, base, grad, factor = pl.pallas_call(
        functools.partial(kernel, reps, n),
        out_shape=(
            pltpu.VMEM(momentum.shape, BF16),
            pltpu.VMEM(w_slow.shape, F32),
            pltpu.VMEM(w_slow.shape, F32),
            pltpu.VMEM((1, 1, d_out), F32),
        ),
        in_specs=[hbm] * 5 + [pl.BlockSpec(memory_space=pltpu.SMEM)],
        out_specs=[pl.BlockSpec(memory_space=pltpu.VMEM)] * 4,
        scratch_shapes=scratch,
        compiler_params=pltpu.CompilerParams(
            collective_id=0, has_side_effects=True, vmem_limit_bytes=34 * 1024 * 1024
        ),
        cost_estimate=pl.CostEstimate(
            flops=2 * n * toks * rows * d_out, bytes_accessed=5 * rows * d_out * 2, transcendentals=0
        ),
    )(tokens, cotangent, w_slow, drift, momentum, partner)
    return moment, (base - grad * factor).astype(BF16)


def solution(mesh):
    spec = P("rep", "fsdp", None)
    return jax.shard_map(
        functools.partial(on_device, mesh.shape["rep"], mesh.shape["fsdp"]),
        mesh=mesh,
        in_specs=(spec, spec, spec, spec, spec, P()),
        out_specs=(spec, spec),
        check_vma=False,
    )
```

```python
import functools

import jax
import jax.numpy as jnp
from jax import lax
from jax.experimental import pallas as pl
from jax.experimental.pallas import tpu as pltpu
from jax.sharding import PartitionSpec as P

MESH = pl.DeviceIdType.MESH
CHUNKS = 4
F32 = jnp.float32
BF16 = jnp.bfloat16


def kernel(reps, n, *refs):
    C = CHUNKS
    (tok, cot, slow, drift, mom, partner, mom_out, base, grad, factor_out) = refs[:10]
    (wv, dv, mv, tokv, cotv, mixsrc, mixin, squares, acc, tokt) = refs[10:20]
    owned = refs[20 : 20 + C]
    (ld, tsend, trecv, crecv, crsend, clsend, asend, arecv, bsend, brecv, qsend, qrecv) = refs[20 + C :]
    me = lax.axis_index("rep")
    z = lax.axis_index("fsdp")
    rows = wv.shape[1]
    cw = wv.shape[2]
    rp = rows // reps
    cd = tokv.shape[2]

    def cols(c):
        return pl.ds(c * cw, cw)

    def load(kind, c):
        src, dst = ((slow, wv), (drift, dv), (mom, mv))[kind]
        return pltpu.make_async_copy(src.at[0, :, cols(c)], dst.at[c], ld.at[kind, c])

    def load_cot(q):
        return pltpu.make_async_copy(cot.at[0, :, cols(q)], cotv.at[q, z], ld.at[3, q])

    def tok_cols(k):
        return pl.ds(pl.multiple_of(k * cd, 128), cd)

    load_tok = pltpu.make_async_copy(tok.at[0, :, tok_cols(z)], tokv.at[z], ld.at[4, 0])

    for c in range(C):
        load(0, c).start()
        load(1, c).start()

    barrier = pltpu.get_barrier_semaphore()
    for d in range(1, n):
        pl.semaphore_signal(barrier, inc=1, device_id=(me, lax.rem(z + d, n)), device_id_type=MESH)

    def greet(d, _):
        pl.semaphore_signal(barrier, inc=1, device_id=(lax.rem(me + d, reps), z), device_id_type=MESH)
        return 0

    lax.fori_loop(1, reps, greet, 0)
    for q in range(C):
        load_cot(q).start()
    load_tok.start()
    for c in range(C):
        load(2, c).start()
    pl.semaphore_wait(barrier, reps - 1 + n - 1)

    def right_copy(q, s, src):
        return pltpu.make_async_remote_copy(
            src_ref=src, dst_ref=cotv.at[q, s], send_sem=crsend.at[q, s], recv_sem=crecv.at[q, s],
            device_id=(me, lax.min(z + 1, n - 1)), device_id_type=MESH)

    def left_copy(q, s, src):
        return pltpu.make_async_remote_copy(
            src_ref=src, dst_ref=cotv.at[q, s], send_sem=clsend.at[q, s], recv_sem=crecv.at[q, s],
            device_id=(me, lax.max(z - 1, 0)), device_id_type=MESH)

    for q in range(C):
        @pl.when(z + 1 < n)
        def _():
            right_copy(q, z, cot.at[0, :, cols(q)]).start()

        @pl.when(z > 0)
        def _():
            left_copy(q, z, cot.at[0, :, cols(q)]).start()

    def tok_copy(d):
        k = lax.rem(z + d, n)
        return pltpu.make_async_remote_copy(
            src_ref=tok.at[0, :, tok_cols(k)], dst_ref=tokv.at[z], send_sem=tsend.at[d], recv_sem=trecv.at[d],
            device_id=(me, k), device_id_type=MESH)

    for d in range(1, n):
        tok_copy(d).start()

    def first_leg(c, d):
        j = lax.rem(me + d, reps)
        return pltpu.make_async_remote_copy(
            src_ref=mixsrc.at[c, j], dst_ref=owned[c].at[me], send_sem=asend.at[c, d], recv_sem=arecv.at[c, d],
            device_id=(j, z), device_id_type=MESH)

    def first_leg_in(c, d):
        s = lax.rem(me + reps - d, reps)
        return pltpu.make_async_remote_copy(
            src_ref=mixsrc.at[c, s], dst_ref=owned[c].at[s], send_sem=asend.at[c, d], recv_sem=arecv.at[c, d],
            device_id=(s, z), device_id_type=MESH)

    def second_leg(c, d):
        j = lax.rem(me + d, reps)
        return pltpu.make_async_remote_copy(
            src_ref=mixsrc.at[c, j], dst_ref=mixin.at[c, me], send_sem=bsend.at[c, d], recv_sem=brecv.at[c, d],
            device_id=(j, z), device_id_type=MESH)

    def second_leg_in(c, d):
        s = lax.rem(me + reps - d, reps)
        return pltpu.make_async_remote_copy(
            src_ref=mixsrc.at[c, s], dst_ref=mixin.at[c, s], send_sem=bsend.at[c, d], recv_sem=brecv.at[c, d],
            device_id=(s, z), device_id_type=MESH)

    def block_rows(j):
        return pl.ds(pl.multiple_of(j * rp, rp), rp)

    def mix_block(c, j):
        part = block_rows(j)
        return (0.5 * (0.7 * dv[c, part, :].astype(F32) - 0.3 * wv[c, part, :].astype(F32))).astype(BF16)

    for c in range(C):
        load(0, c).wait()
        load(1, c).wait()

        def send_block(d, _):
            j = lax.rem(me + d, reps)
            mixsrc[c, j] = mix_block(c, j)
            first_leg(c, d).start()
            return 0

        lax.fori_loop(1, reps, send_block, 0)
        owned[c][me] = mix_block(c, me)

    def turn_round(c):
        def arrived(d, _):
            first_leg_in(c, d).wait_recv()
            first_leg(c, d).wait_send()
            return 0

        lax.fori_loop(1, reps, arrived, 0)

        def send_back(d, _):
            j = lax.rem(me + d, reps)
            mixsrc[c, j] = owned[c][partner[j]]
            second_leg(c, d).start()
            return 0

        lax.fori_loop(1, reps, send_back, 0)
        mixin[c, me] = owned[c][partner[me]]

    def finish_momentum(c):
        load(2, c).wait()

        def arrived(d, _):
            second_leg_in(c, d).wait_recv()
            return 0

        lax.fori_loop(1, reps, arrived, 0)

        def block(j, _):
            part = block_rows(j)
            own = wv[c, part, :].astype(F32)
            moment = (0.5 * mv[c, part, :].astype(F32) + 0.35 * dv[c, part, :].astype(F32) + 0.15 * own
                      + mixin[c, j].astype(F32))
            mom_out[0, part, cols(c)] = moment.astype(BF16)
            base[0, part, cols(c)] = own - moment
            return 0

        lax.fori_loop(0, reps, block, 0)

    tile = 256

    def turn_tokens(s):
        def block(i, _):
            part = pl.ds(pl.multiple_of(i * tile, tile), tile)
            tokt[s, part, :] = tokv[s, :, part].T
            return 0

        lax.fori_loop(0, rows // tile, block, 0)

    def product(q, s, first):
        def block(i, _):
            part = pl.ds(pl.multiple_of(i * tile, tile), tile)
            term = jnp.dot(tokt[s, part, :], cotv[q, s], preferred_element_type=F32).astype(BF16).astype(F32)
            if first:
                grad[0, part, cols(q)] = term
            else:
                grad[0, part, cols(q)] += term
            return 0

        lax.fori_loop(0, rows // tile, block, 0)

    def add_squares(q):
        def block(i, _):
            g = grad[0, pl.ds(pl.multiple_of(i * 64, 64), 64), cols(q)]
            acc[...] += jnp.sum((g * g).reshape(8, 8, cw), axis=0)
            return 0

        lax.fori_loop(0, rows // 64, block, 0)

    def arrive(h, q):
        @pl.when(z - h >= 0)
        def _():
            s = lax.max(z - h, 0)
            right_copy(q, s, cotv.at[q, s]).wait_recv()

            @pl.when(z + 1 < n)
            def _():
                right_copy(q, s, cotv.at[q, s]).start()

        @pl.when(z + h < n)
        def _():
            s = lax.min(z + h, n - 1)
            left_copy(q, s, cotv.at[q, s]).wait_recv()

            @pl.when(z > 0)
            def _():
                left_copy(q, s, cotv.at[q, s]).start()

    def multiply(h, q):
        @pl.when(z - h >= 0)
        def _():
            s = lax.max(z - h, 0)
            if q == 0:
                tok_in(s, h).wait_recv()
                turn_tokens(s)
            product(q, s, False)

        @pl.when(z + h < n)
        def _():
            s = lax.min(z + h, n - 1)
            if q == 0:
                tok_in(s, n - h).wait_recv()
                turn_tokens(s)
            product(q, s, False)

        @pl.when(lax.max(z, n - 1 - z) == h)
        def _():
            add_squares(q)

    def tok_in(s, d):
        return pltpu.make_async_remote_copy(
            src_ref=tokv.at[s], dst_ref=tokv.at[s], send_sem=tsend.at[d], recv_sem=trecv.at[d],
            device_id=(me, s), device_id_type=MESH)

    acc[...] = jnp.zeros_like(acc)
    load_tok.wait()
    turn_tokens(z)
    for q in range(C):
        load_cot(q).wait()
        product(q, z, True)
    for h in range(1, n):
        for q in range(C):
            if h == n - 1 and q == C - 2:
                for c in range(C - 2):
                    finish_momentum(c)
            if h == n - 1 and q == C - 1:
                finish_momentum(C - 2)
            arrive(h, q)
            if h == 1:
                turn_round(q)
            if h > 1:
                multiply(h - 1, q)
            if h == n - 1:
                multiply(h, q)

    part_sum = acc[:, 0:128]
    for k in range(1, cw // 128):
        part_sum = part_sum + acc[:, k * 128 : (k + 1) * 128]
    squares[z] = part_sum

    def squares_copy(d):
        k = lax.rem(z + d, n)
        return pltpu.make_async_remote_copy(
            src_ref=squares.at[z], dst_ref=squares.at[z], send_sem=qsend.at[d], recv_sem=qrecv.at[d],
            device_id=(me, k), device_id_type=MESH)

    for d in range(1, n):
        squares_copy(d).start()
    finish_momentum(C - 1)
    for d in range(1, n):
        s = lax.rem(z + n - d, n)
        pltpu.make_async_remote_copy(
            src_ref=squares.at[s], dst_ref=squares.at[s], send_sem=qsend.at[d], recv_sem=qrecv.at[d],
            device_id=(me, s), device_id_type=MESH).wait_recv()
    total = jnp.sum(jnp.sum(squares[...], axis=0), axis=(0, 1), keepdims=True)
    factor = 0.5 / jnp.sqrt(total / (rows * n * C * cw) + 1e-06)
    factor_out[...] = jnp.broadcast_to(factor[None], factor_out.shape)

    for d in range(1, n):
        tok_copy(d).wait_send()
        squares_copy(d).wait_send()
    for q in range(C):
        for h in range(0, n):
            @pl.when((z - h >= 0) & (z + 1 < n))
            def _():
                s = lax.max(z - h, 0)
                right_copy(q, s, cotv.at[q, s]).wait_send()

            @pl.when((z + h < n) & (z > 0))
            def _():
                s = lax.min(z + h, n - 1)
                left_copy(q, s, cotv.at[q, s]).wait_send()

        def sent(d, _):
            second_leg(q, d).wait_send()
            return 0

        lax.fori_loop(1, reps, sent, 0)


def last_pass(parts, moment, base, grad, factor, mom_out, w_out, held, sem):
    depth = held.shape[1]
    step = 16
    mom_copy = pltpu.make_async_copy(moment, mom_out, sem.at[parts])
    mom_copy.start()
    copies = []
    for k in range(parts):
        def block(i, _):
            part = pl.ds(pl.multiple_of(k * depth + i * step, step), step)
            held[k, pl.ds(pl.multiple_of(i * step, step), step), :] = (
                base[0, part, :] - grad[0, part, :] * factor[0]
            ).astype(BF16)
            return 0

        lax.fori_loop(0, depth // step, block, 0)
        copies.append(pltpu.make_async_copy(held.at[k], w_out.at[0, pl.ds(k * depth, depth), :], sem.at[k]))
        copies[-1].start()
    for copy in copies:
        copy.wait()
    mom_copy.wait()


def on_device(reps, n, tokens, cotangent, w_slow, drift, momentum, partner):
    C = CHUNKS
    _, toks, d_in = tokens.shape
    _, rows, d_out = w_slow.shape
    cw, rp, cd = d_out // C, rows // reps, d_in // n
    hbm = pl.BlockSpec(memory_space=pl.ANY)
    dma = pltpu.SemaphoreType.DMA
    scratch = [
        pltpu.VMEM((C, rows, cw), BF16),
        pltpu.VMEM((C, rows, cw), BF16),
        pltpu.VMEM((C, rows, cw), BF16),
        pltpu.VMEM((n, toks, cd), BF16),
        pltpu.VMEM((C, n, toks, cw), BF16),
        pltpu.VMEM((C, reps, rp, cw), BF16),
        pltpu.VMEM((C, reps, rp, cw), BF16),
        pltpu.VMEM((n, 8, 128), F32),
        pltpu.VMEM((8, cw), F32),
        pltpu.VMEM((n, cd, toks), BF16),
    ]
    scratch += [pltpu.VMEM((reps, rp, cw), BF16) for _ in range(C)]
    scratch += [
        dma((5, C)), dma((n,)), dma((n,)), dma((C, n)), dma((C, n)), dma((C, n)),
        dma((C, reps)), dma((C, reps)), dma((C, reps)), dma((C, reps)), dma((n,)), dma((n,)),
    ]
    moment, base, grad, factor = pl.pallas_call(
        functools.partial(kernel, reps, n),
        out_shape=(
            pltpu.VMEM(momentum.shape, BF16),
            pltpu.VMEM(w_slow.shape, F32),
            pltpu.VMEM(w_slow.shape, F32),
            pltpu.VMEM((1, 1, d_out), F32),
        ),
        in_specs=[hbm] * 5 + [pl.BlockSpec(memory_space=pltpu.SMEM)],
        out_specs=[pl.BlockSpec(memory_space=pltpu.VMEM)] * 4,
        scratch_shapes=scratch,
        compiler_params=pltpu.CompilerParams(
            collective_id=0, has_side_effects=True, vmem_limit_bytes=34 * 1024 * 1024
        ),
        cost_estimate=pl.CostEstimate(
            flops=2 * n * toks * rows * d_out, bytes_accessed=5 * rows * d_out * 2, transcendentals=0
        ),
    )(tokens, cotangent, w_slow, drift, momentum, partner)
    parts = 8
    return pl.pallas_call(
        functools.partial(last_pass, parts),
        out_shape=(jax.ShapeDtypeStruct(momentum.shape, BF16), jax.ShapeDtypeStruct(w_slow.shape, BF16)),
        in_specs=[pl.BlockSpec(memory_space=pltpu.VMEM)] * 4,
        out_specs=(hbm, hbm),
        scratch_shapes=[pltpu.VMEM((parts, rows // parts, d_out), BF16), dma((parts + 1,))],
        compiler_params=pltpu.CompilerParams(vmem_limit_bytes=8 * 1024 * 1024),
        cost_estimate=pl.CostEstimate(flops=2 * rows * d_out, bytes_accessed=4 * rows * d_out, transcendentals=0),
    )(moment, base, grad, factor)


def solution(mesh):
    spec = P("rep", "fsdp", None)
    return jax.shard_map(
        functools.partial(on_device, mesh.shape["rep"], mesh.shape["fsdp"]),
        mesh=mesh,
        in_specs=(spec, spec, spec, spec, spec, P()),
        out_specs=(spec, spec),
        check_vma=False,
    )
```

```python
import functools

import jax
import jax.numpy as jnp
from jax import lax
from jax.experimental import pallas as pl
from jax.experimental.pallas import tpu as pltpu
from jax.sharding import PartitionSpec as P

MESH = pl.DeviceIdType.MESH
CHUNKS = 4
F32 = jnp.float32
BF16 = jnp.bfloat16


def kernel(reps, n, *refs):
    C = CHUNKS
    (tok, cot, slow, drift, mom, partner, mom_out, base, grad, factor_out) = refs[:10]
    (wv, dv, mv, tokv, cotv, mixsrc, mixin, squares, acc, tokt) = refs[10:20]
    owned = refs[20 : 20 + C]
    (ld, tsend, trecv, crecv, crsend, clsend, asend, arecv, bsend, brecv, qsend, qrecv) = refs[20 + C :]
    me = lax.axis_index("rep")
    z = lax.axis_index("fsdp")
    rows = wv.shape[1]
    cw = wv.shape[2]
    rp = rows // reps
    cd = tokv.shape[2]

    bits = reps.bit_length() - 1
    paired = reps == 1 << bits

    def bit(value, i):
        return lax.rem(lax.div(value, 1 << i), 2)

    def to(d):
        if not paired:
            return lax.rem(me + d, reps)
        return sum((bit(me, i) + bit(d, i) - 2 * bit(me, i) * bit(d, i)) * (1 << i) for i in range(bits))

    def source(d):
        return to(d) if paired else lax.rem(me + reps - d, reps)

    def distance(k):
        if not paired or bits < 3:
            return k
        d = lax.rem(k, reps - 1) + 1
        return d + 2 * (bit(d, 1) - bit(d, 2)) * lax.rem(me, 2)

    def cols(c):
        return pl.ds(c * cw, cw)

    def load(kind, c):
        src, dst = ((slow, wv), (drift, dv), (mom, mv))[kind]
        return pltpu.make_async_copy(src.at[0, :, cols(c)], dst.at[c], ld.at[kind, c])

    def load_cot(q):
        return pltpu.make_async_copy(cot.at[0, :, cols(q)], cotv.at[q, z], ld.at[3, q])

    def tok_cols(k):
        return pl.ds(pl.multiple_of(k * cd, 128), cd)

    load_tok = pltpu.make_async_copy(tok.at[0, :, tok_cols(z)], tokv.at[z], ld.at[4, 0])

    for c in range(C):
        load(0, c).start()
        load(1, c).start()

    barrier = pltpu.get_barrier_semaphore()
    for d in range(1, n):
        pl.semaphore_signal(barrier, inc=1, device_id=(me, lax.rem(z + d, n)), device_id_type=MESH)

    def greet(d, _):
        pl.semaphore_signal(barrier, inc=1, device_id=(lax.rem(me + d, reps), z), device_id_type=MESH)
        return 0

    lax.fori_loop(1, reps, greet, 0)
    for q in range(C):
        load_cot(q).start()
    load_tok.start()
    for c in range(C):
        load(2, c).start()
    pl.semaphore_wait(barrier, reps - 1 + n - 1)

    def right_copy(q, s, src):
        return pltpu.make_async_remote_copy(
            src_ref=src, dst_ref=cotv.at[q, s], send_sem=crsend.at[q, s], recv_sem=crecv.at[q, s],
            device_id=(me, lax.min(z + 1, n - 1)), device_id_type=MESH)

    def left_copy(q, s, src):
        return pltpu.make_async_remote_copy(
            src_ref=src, dst_ref=cotv.at[q, s], send_sem=clsend.at[q, s], recv_sem=crecv.at[q, s],
            device_id=(me, lax.max(z - 1, 0)), device_id_type=MESH)

    for q in range(C):
        @pl.when(z + 1 < n)
        def _():
            right_copy(q, z, cot.at[0, :, cols(q)]).start()

        @pl.when(z > 0)
        def _():
            left_copy(q, z, cot.at[0, :, cols(q)]).start()

    def tok_copy(d):
        k = lax.rem(z + d, n)
        return pltpu.make_async_remote_copy(
            src_ref=tok.at[0, :, tok_cols(k)], dst_ref=tokv.at[z], send_sem=tsend.at[d], recv_sem=trecv.at[d],
            device_id=(me, k), device_id_type=MESH)

    for d in range(1, n):
        tok_copy(d).start()

    def first_leg(c, d):
        j = to(d)
        return pltpu.make_async_remote_copy(
            src_ref=mixsrc.at[c, j], dst_ref=owned[c].at[me], send_sem=asend.at[c, d], recv_sem=arecv.at[c, d],
            device_id=(j, z), device_id_type=MESH)

    def first_leg_in(c, d):
        s = source(d)
        return pltpu.make_async_remote_copy(
            src_ref=mixsrc.at[c, s], dst_ref=owned[c].at[s], send_sem=asend.at[c, d], recv_sem=arecv.at[c, d],
            device_id=(s, z), device_id_type=MESH)

    def second_leg(c, d):
        j = to(d)
        return pltpu.make_async_remote_copy(
            src_ref=mixsrc.at[c, j], dst_ref=mixin.at[c, me], send_sem=bsend.at[c, d], recv_sem=brecv.at[c, d],
            device_id=(j, z), device_id_type=MESH)

    def second_leg_in(c, d):
        s = source(d)
        return pltpu.make_async_remote_copy(
            src_ref=mixsrc.at[c, s], dst_ref=mixin.at[c, s], send_sem=bsend.at[c, d], recv_sem=brecv.at[c, d],
            device_id=(s, z), device_id_type=MESH)

    def block_rows(j):
        return pl.ds(pl.multiple_of(j * rp, rp), rp)

    def mix_block(c, j):
        part = block_rows(j)
        return (0.5 * (0.7 * dv[c, part, :].astype(F32) - 0.3 * wv[c, part, :].astype(F32))).astype(BF16)

    for c in range(C):
        load(0, c).wait()
        load(1, c).wait()

        def send_block(k, _):
            d = distance(k)
            j = to(d)
            mixsrc[c, j] = mix_block(c, j)
            first_leg(c, d).start()
            return 0

        lax.fori_loop(1, reps, send_block, 0)
        owned[c][me] = mix_block(c, me)

    def turn_round(c):
        def arrived(d, _):
            first_leg_in(c, d).wait_recv()
            first_leg(c, d).wait_send()
            return 0

        lax.fori_loop(1, reps, arrived, 0)

        def send_back(k, _):
            d = distance(k)
            j = to(d)
            mixsrc[c, j] = owned[c][partner[j]]
            second_leg(c, d).start()
            return 0

        lax.fori_loop(1, reps, send_back, 0)
        mixin[c, me] = owned[c][partner[me]]

    def finish_momentum(c):
        load(2, c).wait()

        def arrived(d, _):
            second_leg_in(c, d).wait_recv()
            return 0

        lax.fori_loop(1, reps, arrived, 0)

        def block(j, _):
            part = block_rows(j)
            own = wv[c, part, :].astype(F32)
            moment = (0.5 * mv[c, part, :].astype(F32) + 0.35 * dv[c, part, :].astype(F32) + 0.15 * own
                      + mixin[c, j].astype(F32))
            mom_out[0, part, cols(c)] = moment.astype(BF16)
            base[0, part, cols(c)] = own - moment
            return 0

        lax.fori_loop(0, reps, block, 0)

    tile = 256

    def turn_tokens(s):
        def block(i, _):
            part = pl.ds(pl.multiple_of(i * tile, tile), tile)
            tokt[s, part, :] = tokv[s, :, part].T
            return 0

        lax.fori_loop(0, rows // tile, block, 0)

    def product(q, s, first):
        def block(i, _):
            part = pl.ds(pl.multiple_of(i * tile, tile), tile)
            term = jnp.dot(tokt[s, part, :], cotv[q, s], preferred_element_type=F32).astype(BF16).astype(F32)
            if first:
                grad[0, part, cols(q)] = term
            else:
                grad[0, part, cols(q)] += term
            return 0

        lax.fori_loop(0, rows // tile, block, 0)

    def add_squares(q):
        def block(i, _):
            g = grad[0, pl.ds(pl.multiple_of(i * 64, 64), 64), cols(q)]
            acc[...] += jnp.sum((g * g).reshape(8, 8, cw), axis=0)
            return 0

        lax.fori_loop(0, rows // 64, block, 0)

    def arrive(h, q):
        @pl.when(z - h >= 0)
        def _():
            s = lax.max(z - h, 0)
            right_copy(q, s, cotv.at[q, s]).wait_recv()

            @pl.when(z + 1 < n)
            def _():
                right_copy(q, s, cotv.at[q, s]).start()

        @pl.when(z + h < n)
        def _():
            s = lax.min(z + h, n - 1)
            left_copy(q, s, cotv.at[q, s]).wait_recv()

            @pl.when(z > 0)
            def _():
                left_copy(q, s, cotv.at[q, s]).start()

    def multiply(h, q):
        @pl.when(z - h >= 0)
        def _():
            s = lax.max(z - h, 0)
            if q == 0:
                tok_in(s, h).wait_recv()
                turn_tokens(s)
            product(q, s, False)

        @pl.when(z + h < n)
        def _():
            s = lax.min(z + h, n - 1)
            if q == 0:
                tok_in(s, n - h).wait_recv()
                turn_tokens(s)
            product(q, s, False)

        @pl.when(lax.max(z, n - 1 - z) == h)
        def _():
            add_squares(q)

    def tok_in(s, d):
        return pltpu.make_async_remote_copy(
            src_ref=tokv.at[s], dst_ref=tokv.at[s], send_sem=tsend.at[d], recv_sem=trecv.at[d],
            device_id=(me, s), device_id_type=MESH)

    acc[...] = jnp.zeros_like(acc)
    load_tok.wait()
    turn_tokens(z)
    for q in range(C):
        load_cot(q).wait()
        product(q, z, True)
    for h in range(1, n):
        for q in range(C):
            if h == n - 1 and q == C - 2:
                for c in range(C - 2):
                    finish_momentum(c)
            if h == n - 1 and q == C - 1:
                finish_momentum(C - 2)
            arrive(h, q)
            if h == 1:
                turn_round(q)
            if h > 1:
                multiply(h - 1, q)
            if h == n - 1:
                multiply(h, q)

    part_sum = acc[:, 0:128]
    for k in range(1, cw // 128):
        part_sum = part_sum + acc[:, k * 128 : (k + 1) * 128]
    squares[z] = part_sum

    def squares_copy(d):
        k = lax.rem(z + d, n)
        return pltpu.make_async_remote_copy(
            src_ref=squares.at[z], dst_ref=squares.at[z], send_sem=qsend.at[d], recv_sem=qrecv.at[d],
            device_id=(me, k), device_id_type=MESH)

    for d in range(1, n):
        squares_copy(d).start()
    finish_momentum(C - 1)
    for d in range(1, n):
        s = lax.rem(z + n - d, n)
        pltpu.make_async_remote_copy(
            src_ref=squares.at[s], dst_ref=squares.at[s], send_sem=qsend.at[d], recv_sem=qrecv.at[d],
            device_id=(me, s), device_id_type=MESH).wait_recv()
    total = jnp.sum(jnp.sum(squares[...], axis=0), axis=(0, 1), keepdims=True)
    factor = 0.5 / jnp.sqrt(total / (rows * n * C * cw) + 1e-06)
    factor_out[...] = jnp.broadcast_to(factor[None], factor_out.shape)

    for d in range(1, n):
        tok_copy(d).wait_send()
        squares_copy(d).wait_send()
    for q in range(C):
        for h in range(0, n):
            @pl.when((z - h >= 0) & (z + 1 < n))
            def _():
                s = lax.max(z - h, 0)
                right_copy(q, s, cotv.at[q, s]).wait_send()

            @pl.when((z + h < n) & (z > 0))
            def _():
                s = lax.min(z + h, n - 1)
                left_copy(q, s, cotv.at[q, s]).wait_send()

        def sent(d, _):
            second_leg(q, d).wait_send()
            return 0

        lax.fori_loop(1, reps, sent, 0)


def last_pass(parts, moment, base, grad, factor, mom_out, w_out, held, sem):
    depth = held.shape[1]
    step = 16
    mom_copy = pltpu.make_async_copy(moment, mom_out, sem.at[parts])
    mom_copy.start()
    copies = []
    for k in range(parts):
        def block(i, _):
            part = pl.ds(pl.multiple_of(k * depth + i * step, step), step)
            held[k, pl.ds(pl.multiple_of(i * step, step), step), :] = (
                base[0, part, :] - grad[0, part, :] * factor[0]
            ).astype(BF16)
            return 0

        lax.fori_loop(0, depth // step, block, 0)
        copies.append(pltpu.make_async_copy(held.at[k], w_out.at[0, pl.ds(k * depth, depth), :], sem.at[k]))
        copies[-1].start()
    for copy in copies:
        copy.wait()
    mom_copy.wait()


def on_device(reps, n, tokens, cotangent, w_slow, drift, momentum, partner):
    C = CHUNKS
    _, toks, d_in = tokens.shape
    _, rows, d_out = w_slow.shape
    cw, rp, cd = d_out // C, rows // reps, d_in // n
    hbm = pl.BlockSpec(memory_space=pl.ANY)
    dma = pltpu.SemaphoreType.DMA
    scratch = [
        pltpu.VMEM((C, rows, cw), BF16),
        pltpu.VMEM((C, rows, cw), BF16),
        pltpu.VMEM((C, rows, cw), BF16),
        pltpu.VMEM((n, toks, cd), BF16),
        pltpu.VMEM((C, n, toks, cw), BF16),
        pltpu.VMEM((C, reps, rp, cw), BF16),
        pltpu.VMEM((C, reps, rp, cw), BF16),
        pltpu.VMEM((n, 8, 128), F32),
        pltpu.VMEM((8, cw), F32),
        pltpu.VMEM((n, cd, toks), BF16),
    ]
    scratch += [pltpu.VMEM((reps, rp, cw), BF16) for _ in range(C)]
    scratch += [
        dma((5, C)), dma((n,)), dma((n,)), dma((C, n)), dma((C, n)), dma((C, n)),
        dma((C, reps)), dma((C, reps)), dma((C, reps)), dma((C, reps)), dma((n,)), dma((n,)),
    ]
    moment, base, grad, factor = pl.pallas_call(
        functools.partial(kernel, reps, n),
        out_shape=(
            pltpu.VMEM(momentum.shape, BF16),
            pltpu.VMEM(w_slow.shape, F32),
            pltpu.VMEM(w_slow.shape, F32),
            pltpu.VMEM((1, 1, d_out), F32),
        ),
        in_specs=[hbm] * 5 + [pl.BlockSpec(memory_space=pltpu.SMEM)],
        out_specs=[pl.BlockSpec(memory_space=pltpu.VMEM)] * 4,
        scratch_shapes=scratch,
        compiler_params=pltpu.CompilerParams(
            collective_id=0, has_side_effects=True, vmem_limit_bytes=34 * 1024 * 1024
        ),
        cost_estimate=pl.CostEstimate(
            flops=2 * n * toks * rows * d_out, bytes_accessed=5 * rows * d_out * 2, transcendentals=0
        ),
    )(tokens, cotangent, w_slow, drift, momentum, partner)
    parts = 8
    return pl.pallas_call(
        functools.partial(last_pass, parts),
        out_shape=(jax.ShapeDtypeStruct(momentum.shape, BF16), jax.ShapeDtypeStruct(w_slow.shape, BF16)),
        in_specs=[pl.BlockSpec(memory_space=pltpu.VMEM)] * 4,
        out_specs=(hbm, hbm),
        scratch_shapes=[pltpu.VMEM((parts, rows // parts, d_out), BF16), dma((parts + 1,))],
        compiler_params=pltpu.CompilerParams(vmem_limit_bytes=8 * 1024 * 1024),
        cost_estimate=pl.CostEstimate(flops=2 * rows * d_out, bytes_accessed=4 * rows * d_out, transcendentals=0),
    )(moment, base, grad, factor)


def solution(mesh):
    spec = P("rep", "fsdp", None)
    return jax.shard_map(
        functools.partial(on_device, mesh.shape["rep"], mesh.shape["fsdp"]),
        mesh=mesh,
        in_specs=(spec, spec, spec, spec, spec, P()),
        out_specs=(spec, spec),
        check_vma=False,
    )
```

```python
import functools

import jax
import jax.numpy as jnp
from jax import lax
from jax.experimental import pallas as pl
from jax.experimental.pallas import tpu as pltpu
from jax.sharding import PartitionSpec as P

MESH = pl.DeviceIdType.MESH
CHUNKS = 4
F32 = jnp.float32
BF16 = jnp.bfloat16


def kernel(reps, n, *refs):
    C = CHUNKS
    (tok, cot, slow, drift, mom, partner, mom_out, base, grad, factor_out) = refs[:10]
    (wv, dv, mv, tokv, cotv, mixsrc, mixin, squares, acc, tokt) = refs[10:20]
    owned = refs[20 : 20 + C]
    (ld, tsend, trecv, crecv, crsend, clsend, asend, arecv, bsend, brecv, qsend, qrecv) = refs[20 + C :]
    me = lax.axis_index("rep")
    z = lax.axis_index("fsdp")
    rows = wv.shape[1]
    cw = wv.shape[2]
    rp = rows // reps
    cd = tokv.shape[2]

    bits = reps.bit_length() - 1
    paired = reps == 1 << bits

    def bit(value, i):
        return lax.rem(lax.div(value, 1 << i), 2)

    def to(d):
        if not paired:
            return lax.rem(me + d, reps)
        return sum((bit(me, i) + bit(d, i) - 2 * bit(me, i) * bit(d, i)) * (1 << i) for i in range(bits))

    def source(d):
        return to(d) if paired else lax.rem(me + reps - d, reps)

    def distance(k):
        if not paired or bits < 3:
            return k
        d = lax.rem(k, reps - 1) + 1
        return d + 2 * (bit(d, 1) - bit(d, 2)) * lax.rem(me, 2)

    def cols(c):
        return pl.ds(c * cw, cw)

    def load(kind, c):
        src, dst = ((slow, wv), (drift, dv), (mom, mv))[kind]
        return pltpu.make_async_copy(src.at[0, :, cols(c)], dst.at[c], ld.at[kind, c])

    def load_cot(q):
        return pltpu.make_async_copy(cot.at[0, :, cols(q)], cotv.at[q, z], ld.at[3, q])

    def tok_cols(k):
        return pl.ds(pl.multiple_of(k * cd, 128), cd)

    load_tok = pltpu.make_async_copy(tok.at[0, :, tok_cols(z)], tokv.at[z], ld.at[4, 0])

    for c in range(C):
        load(0, c).start()
        load(1, c).start()

    barrier = pltpu.get_barrier_semaphore()
    for d in range(1, n):
        pl.semaphore_signal(barrier, inc=1, device_id=(me, lax.rem(z + d, n)), device_id_type=MESH)

    def greet(d, _):
        pl.semaphore_signal(barrier, inc=1, device_id=(lax.rem(me + d, reps), z), device_id_type=MESH)
        return 0

    lax.fori_loop(1, reps, greet, 0)
    for q in range(C):
        load_cot(q).start()
    load_tok.start()
    for c in range(C):
        load(2, c).start()
    pl.semaphore_wait(barrier, reps - 1 + n - 1)

    def right_copy(q, s, src):
        return pltpu.make_async_remote_copy(
            src_ref=src, dst_ref=cotv.at[q, s], send_sem=crsend.at[q, s], recv_sem=crecv.at[q, s],
            device_id=(me, lax.min(z + 1, n - 1)), device_id_type=MESH)

    def left_copy(q, s, src):
        return pltpu.make_async_remote_copy(
            src_ref=src, dst_ref=cotv.at[q, s], send_sem=clsend.at[q, s], recv_sem=crecv.at[q, s],
            device_id=(me, lax.max(z - 1, 0)), device_id_type=MESH)

    for q in range(C):
        @pl.when(z + 1 < n)
        def _():
            right_copy(q, z, cot.at[0, :, cols(q)]).start()

        @pl.when(z > 0)
        def _():
            left_copy(q, z, cot.at[0, :, cols(q)]).start()

    def tok_copy(d):
        k = lax.rem(z + d, n)
        return pltpu.make_async_remote_copy(
            src_ref=tok.at[0, :, tok_cols(k)], dst_ref=tokv.at[z], send_sem=tsend.at[d], recv_sem=trecv.at[d],
            device_id=(me, k), device_id_type=MESH)

    def first_leg(c, d):
        j = to(d)
        return pltpu.make_async_remote_copy(
            src_ref=mixsrc.at[c, j], dst_ref=owned[c].at[me], send_sem=asend.at[c, d], recv_sem=arecv.at[c, d],
            device_id=(j, z), device_id_type=MESH)

    def first_leg_in(c, d):
        s = source(d)
        return pltpu.make_async_remote_copy(
            src_ref=mixsrc.at[c, s], dst_ref=owned[c].at[s], send_sem=asend.at[c, d], recv_sem=arecv.at[c, d],
            device_id=(s, z), device_id_type=MESH)

    def second_leg(c, d):
        j = to(d)
        return pltpu.make_async_remote_copy(
            src_ref=mixsrc.at[c, j], dst_ref=mixin.at[c, me], send_sem=bsend.at[c, d], recv_sem=brecv.at[c, d],
            device_id=(j, z), device_id_type=MESH)

    def second_leg_in(c, d):
        s = source(d)
        return pltpu.make_async_remote_copy(
            src_ref=mixsrc.at[c, s], dst_ref=mixin.at[c, s], send_sem=bsend.at[c, d], recv_sem=brecv.at[c, d],
            device_id=(s, z), device_id_type=MESH)

    def block_rows(j):
        return pl.ds(pl.multiple_of(j * rp, rp), rp)

    def mix_block(c, j):
        part = block_rows(j)
        return (0.5 * (0.7 * dv[c, part, :].astype(F32) - 0.3 * wv[c, part, :].astype(F32))).astype(BF16)

    def send_mix(c):
        load(0, c).wait()
        load(1, c).wait()

        def send_block(k, _):
            d = distance(k)
            j = to(d)
            mixsrc[c, j] = mix_block(c, j)
            first_leg(c, d).start()
            return 0

        lax.fori_loop(1, reps, send_block, 0)
        owned[c][me] = mix_block(c, me)

    def turn_round(c):
        def arrived(d, _):
            first_leg_in(c, d).wait_recv()
            first_leg(c, d).wait_send()
            return 0

        lax.fori_loop(1, reps, arrived, 0)

        def send_back(k, _):
            d = distance(k)
            j = to(d)
            mixsrc[c, j] = owned[c][partner[j]]
            second_leg(c, d).start()
            return 0

        lax.fori_loop(1, reps, send_back, 0)
        mixin[c, me] = owned[c][partner[me]]

    def finish_momentum(c):
        load(2, c).wait()

        def arrived(d, _):
            second_leg_in(c, d).wait_recv()
            return 0

        lax.fori_loop(1, reps, arrived, 0)

        def block(j, _):
            part = block_rows(j)
            own = wv[c, part, :].astype(F32)
            moment = (0.5 * mv[c, part, :].astype(F32) + 0.35 * dv[c, part, :].astype(F32) + 0.15 * own
                      + mixin[c, j].astype(F32))
            mom_out[0, part, cols(c)] = moment.astype(BF16)
            base[0, part, cols(c)] = own - moment
            return 0

        lax.fori_loop(0, reps, block, 0)

    tile = 256

    def turn_tokens(s):
        def block(i, _):
            part = pl.ds(pl.multiple_of(i * tile, tile), tile)
            tokt[s, part, :] = tokv[s, :, part].T
            return 0

        lax.fori_loop(0, rows // tile, block, 0)

    def product(q, s, first):
        def block(i, _):
            part = pl.ds(pl.multiple_of(i * tile, tile), tile)
            term = jnp.dot(tokt[s, part, :], cotv[q, s], preferred_element_type=F32).astype(BF16).astype(F32)
            if first:
                grad[0, part, cols(q)] = term
            else:
                grad[0, part, cols(q)] += term
            return 0

        lax.fori_loop(0, rows // tile, block, 0)

    def add_squares(q):
        def block(i, _):
            g = grad[0, pl.ds(pl.multiple_of(i * 64, 64), 64), cols(q)]
            acc[...] += jnp.sum((g * g).reshape(8, 8, cw), axis=0)
            return 0

        lax.fori_loop(0, rows // 64, block, 0)

    def arrive(h, q):
        @pl.when(z - h >= 0)
        def _():
            s = lax.max(z - h, 0)
            right_copy(q, s, cotv.at[q, s]).wait_recv()

            @pl.when(z + 1 < n)
            def _():
                right_copy(q, s, cotv.at[q, s]).start()

        @pl.when(z + h < n)
        def _():
            s = lax.min(z + h, n - 1)
            left_copy(q, s, cotv.at[q, s]).wait_recv()

            @pl.when(z > 0)
            def _():
                left_copy(q, s, cotv.at[q, s]).start()

    def multiply(h, q):
        @pl.when(z - h >= 0)
        def _():
            s = lax.max(z - h, 0)
            if q == 0:
                tok_in(s, h).wait_recv()
                turn_tokens(s)
            product(q, s, False)

        @pl.when(z + h < n)
        def _():
            s = lax.min(z + h, n - 1)
            if q == 0:
                tok_in(s, n - h).wait_recv()
                turn_tokens(s)
            product(q, s, False)

        @pl.when(lax.max(z, n - 1 - z) == h)
        def _():
            add_squares(q)

    def tok_in(s, d):
        return pltpu.make_async_remote_copy(
            src_ref=tokv.at[s], dst_ref=tokv.at[s], send_sem=tsend.at[d], recv_sem=trecv.at[d],
            device_id=(me, s), device_id_type=MESH)

    send_mix(0)
    send_mix(1)
    acc[...] = jnp.zeros_like(acc)
    load_tok.wait()
    turn_tokens(z)
    for q in range(C):
        arrive(1, q)
        if q % 2 == 1 and 2 + q // 2 < C:
            send_mix(2 + q // 2)
    for d in range(1, n):
        tok_copy(d).start()
    turn_round(0)
    for q in range(C):
        load_cot(q).wait()
        product(q, z, True)
        if n > 3:
            arrive(2, q)
        if q + 1 < C:
            turn_round(q + 1)
    for h in range(3, n - 1):
        for q in range(C):
            arrive(h, q)
    for h in range(1, n - 1):
        for q in range(C):
            multiply(h, q)
    for q in range(C):
        if q == C - 2:
            for c in range(C - 2):
                finish_momentum(c)
        if q == C - 1:
            finish_momentum(C - 2)
        arrive(n - 1, q)
        multiply(n - 1, q)

    part_sum = acc[:, 0:128]
    for k in range(1, cw // 128):
        part_sum = part_sum + acc[:, k * 128 : (k + 1) * 128]
    squares[z] = part_sum

    def squares_copy(d):
        k = lax.rem(z + d, n)
        return pltpu.make_async_remote_copy(
            src_ref=squares.at[z], dst_ref=squares.at[z], send_sem=qsend.at[d], recv_sem=qrecv.at[d],
            device_id=(me, k), device_id_type=MESH)

    for d in range(1, n):
        squares_copy(d).start()
    finish_momentum(C - 1)
    for d in range(1, n):
        s = lax.rem(z + n - d, n)
        pltpu.make_async_remote_copy(
            src_ref=squares.at[s], dst_ref=squares.at[s], send_sem=qsend.at[d], recv_sem=qrecv.at[d],
            device_id=(me, s), device_id_type=MESH).wait_recv()
    total = jnp.sum(jnp.sum(squares[...], axis=0), axis=(0, 1), keepdims=True)
    factor = 0.5 / jnp.sqrt(total / (rows * n * C * cw) + 1e-06)
    factor_out[...] = jnp.broadcast_to(factor[None], factor_out.shape)

    for d in range(1, n):
        tok_copy(d).wait_send()
        squares_copy(d).wait_send()
    for q in range(C):
        for h in range(0, n):
            @pl.when((z - h >= 0) & (z + 1 < n))
            def _():
                s = lax.max(z - h, 0)
                right_copy(q, s, cotv.at[q, s]).wait_send()

            @pl.when((z + h < n) & (z > 0))
            def _():
                s = lax.min(z + h, n - 1)
                left_copy(q, s, cotv.at[q, s]).wait_send()

        def sent(d, _):
            second_leg(q, d).wait_send()
            return 0

        lax.fori_loop(1, reps, sent, 0)


def last_pass(parts, moment, base, grad, factor, mom_out, w_out, held, sem):
    depth = held.shape[1]
    step = 16
    mom_copy = pltpu.make_async_copy(moment, mom_out, sem.at[parts])
    mom_copy.start()
    copies = []
    for k in range(parts):
        def block(i, _):
            part = pl.ds(pl.multiple_of(k * depth + i * step, step), step)
            held[k, pl.ds(pl.multiple_of(i * step, step), step), :] = (
                base[0, part, :] - grad[0, part, :] * factor[0]
            ).astype(BF16)
            return 0

        lax.fori_loop(0, depth // step, block, 0)
        copies.append(pltpu.make_async_copy(held.at[k], w_out.at[0, pl.ds(k * depth, depth), :], sem.at[k]))
        copies[-1].start()
    for copy in copies:
        copy.wait()
    mom_copy.wait()


def on_device(reps, n, tokens, cotangent, w_slow, drift, momentum, partner):
    C = CHUNKS
    _, toks, d_in = tokens.shape
    _, rows, d_out = w_slow.shape
    cw, rp, cd = d_out // C, rows // reps, d_in // n
    hbm = pl.BlockSpec(memory_space=pl.ANY)
    dma = pltpu.SemaphoreType.DMA
    scratch = [
        pltpu.VMEM((C, rows, cw), BF16),
        pltpu.VMEM((C, rows, cw), BF16),
        pltpu.VMEM((C, rows, cw), BF16),
        pltpu.VMEM((n, toks, cd), BF16),
        pltpu.VMEM((C, n, toks, cw), BF16),
        pltpu.VMEM((C, reps, rp, cw), BF16),
        pltpu.VMEM((C, reps, rp, cw), BF16),
        pltpu.VMEM((n, 8, 128), F32),
        pltpu.VMEM((8, cw), F32),
        pltpu.VMEM((n, cd, toks), BF16),
    ]
    scratch += [pltpu.VMEM((reps, rp, cw), BF16) for _ in range(C)]
    scratch += [
        dma((5, C)), dma((n,)), dma((n,)), dma((C, n)), dma((C, n)), dma((C, n)),
        dma((C, reps)), dma((C, reps)), dma((C, reps)), dma((C, reps)), dma((n,)), dma((n,)),
    ]
    moment, base, grad, factor = pl.pallas_call(
        functools.partial(kernel, reps, n),
        out_shape=(
            pltpu.VMEM(momentum.shape, BF16),
            pltpu.VMEM(w_slow.shape, F32),
            pltpu.VMEM(w_slow.shape, F32),
            pltpu.VMEM((1, 1, d_out), F32),
        ),
        in_specs=[hbm] * 5 + [pl.BlockSpec(memory_space=pltpu.SMEM)],
        out_specs=[pl.BlockSpec(memory_space=pltpu.VMEM)] * 4,
        scratch_shapes=scratch,
        compiler_params=pltpu.CompilerParams(
            collective_id=0, has_side_effects=True, vmem_limit_bytes=34 * 1024 * 1024
        ),
        cost_estimate=pl.CostEstimate(
            flops=2 * n * toks * rows * d_out, bytes_accessed=5 * rows * d_out * 2, transcendentals=0
        ),
    )(tokens, cotangent, w_slow, drift, momentum, partner)
    parts = 8
    return pl.pallas_call(
        functools.partial(last_pass, parts),
        out_shape=(jax.ShapeDtypeStruct(momentum.shape, BF16), jax.ShapeDtypeStruct(w_slow.shape, BF16)),
        in_specs=[pl.BlockSpec(memory_space=pltpu.VMEM)] * 4,
        out_specs=(hbm, hbm),
        scratch_shapes=[pltpu.VMEM((parts, rows // parts, d_out), BF16), dma((parts + 1,))],
        compiler_params=pltpu.CompilerParams(vmem_limit_bytes=8 * 1024 * 1024),
        cost_estimate=pl.CostEstimate(flops=2 * rows * d_out, bytes_accessed=4 * rows * d_out, transcendentals=0),
    )(moment, base, grad, factor)


def solution(mesh):
    spec = P("rep", "fsdp", None)
    return jax.shard_map(
        functools.partial(on_device, mesh.shape["rep"], mesh.shape["fsdp"]),
        mesh=mesh,
        in_specs=(spec, spec, spec, spec, spec, P()),
        out_specs=(spec, spec),
        check_vma=False,
    )
```

```python
import functools

import jax
import jax.numpy as jnp
from jax import lax
from jax.experimental import pallas as pl
from jax.experimental.pallas import tpu as pltpu
from jax.sharding import PartitionSpec as P

MESH = pl.DeviceIdType.MESH
CHUNKS = 4
F32 = jnp.float32
BF16 = jnp.bfloat16


def kernel(reps, n, *refs):
    C = CHUNKS
    (tok, cot, slow, drift, mom, partner, mom_out, base, grad, factor_out) = refs[:10]
    (wv, dv, mv, tokv, cotv, mixsrc, mixin, squares, acc, tokt) = refs[10:20]
    owned = refs[20 : 20 + C]
    (ld, tsend, trecv, crecv, crsend, clsend, asend, arecv, bsend, brecv, qsend, qrecv) = refs[20 + C :]
    me = lax.axis_index("rep")
    z = lax.axis_index("fsdp")
    rows = wv.shape[1]
    cw = wv.shape[2]
    rp = rows // reps
    cd = tokv.shape[2]

    bits = reps.bit_length() - 1
    paired = reps == 1 << bits

    def bit(value, i):
        return lax.rem(lax.div(value, 1 << i), 2)

    def to(d):
        if not paired:
            return lax.rem(me + d, reps)
        return sum((bit(me, i) + bit(d, i) - 2 * bit(me, i) * bit(d, i)) * (1 << i) for i in range(bits))

    def source(d):
        return to(d) if paired else lax.rem(me + reps - d, reps)

    def distance(k):
        if not paired or bits < 3:
            return k
        d = lax.rem(k, reps - 1) + 1
        return d + 2 * (bit(d, 1) - bit(d, 2)) * lax.rem(me, 2)

    def cols(c):
        return pl.ds(c * cw, cw)

    def load(kind, c):
        src, dst = ((slow, wv), (drift, dv), (mom, mv))[kind]
        return pltpu.make_async_copy(src.at[0, :, cols(c)], dst.at[c], ld.at[kind, c])

    def load_cot(q):
        return pltpu.make_async_copy(cot.at[0, :, cols(q)], cotv.at[q, z], ld.at[3, q])

    def tok_cols(k):
        return pl.ds(pl.multiple_of(k * cd, 128), cd)

    load_tok = pltpu.make_async_copy(tok.at[0, :, tok_cols(z)], tokv.at[z], ld.at[4, 0])

    for c in range(C):
        load(0, c).start()
        load(1, c).start()

    barrier = pltpu.get_barrier_semaphore()
    for d in range(1, n):
        pl.semaphore_signal(barrier, inc=1, device_id=(me, lax.rem(z + d, n)), device_id_type=MESH)

    def greet(d, _):
        pl.semaphore_signal(barrier, inc=1, device_id=(lax.rem(me + d, reps), z), device_id_type=MESH)
        return 0

    lax.fori_loop(1, reps, greet, 0)
    for q in range(C):
        load_cot(q).start()
    load_tok.start()
    for c in range(C):
        load(2, c).start()
    pl.semaphore_wait(barrier, reps - 1 + n - 1)

    def right_copy(q, s, src):
        return pltpu.make_async_remote_copy(
            src_ref=src, dst_ref=cotv.at[q, s], send_sem=crsend.at[q, s], recv_sem=crecv.at[q, s],
            device_id=(me, lax.min(z + 1, n - 1)), device_id_type=MESH)

    def left_copy(q, s, src):
        return pltpu.make_async_remote_copy(
            src_ref=src, dst_ref=cotv.at[q, s], send_sem=clsend.at[q, s], recv_sem=crecv.at[q, s],
            device_id=(me, lax.max(z - 1, 0)), device_id_type=MESH)

    def tok_copy(d):
        k = lax.rem(z + d, n)
        return pltpu.make_async_remote_copy(
            src_ref=tok.at[0, :, tok_cols(k)], dst_ref=tokv.at[z], send_sem=tsend.at[d], recv_sem=trecv.at[d],
            device_id=(me, k), device_id_type=MESH)

    for d in range(1, n):
        tok_copy(d).start()

    for q in range(C):
        @pl.when(z + 1 < n)
        def _():
            right_copy(q, z, cot.at[0, :, cols(q)]).start()

        @pl.when(z > 0)
        def _():
            left_copy(q, z, cot.at[0, :, cols(q)]).start()

    def first_leg(c, d):
        j = to(d)
        return pltpu.make_async_remote_copy(
            src_ref=mixsrc.at[c, j], dst_ref=owned[c].at[me], send_sem=asend.at[c, d], recv_sem=arecv.at[c, d],
            device_id=(j, z), device_id_type=MESH)

    def first_leg_in(c, d):
        s = source(d)
        return pltpu.make_async_remote_copy(
            src_ref=mixsrc.at[c, s], dst_ref=owned[c].at[s], send_sem=asend.at[c, d], recv_sem=arecv.at[c, d],
            device_id=(s, z), device_id_type=MESH)

    def second_leg(c, d):
        j = to(d)
        return pltpu.make_async_remote_copy(
            src_ref=mixsrc.at[c, j], dst_ref=mixin.at[c, me], send_sem=bsend.at[c, d], recv_sem=brecv.at[c, d],
            device_id=(j, z), device_id_type=MESH)

    def second_leg_in(c, d):
        s = source(d)
        return pltpu.make_async_remote_copy(
            src_ref=mixsrc.at[c, s], dst_ref=mixin.at[c, s], send_sem=bsend.at[c, d], recv_sem=brecv.at[c, d],
            device_id=(s, z), device_id_type=MESH)

    def block_rows(j):
        return pl.ds(pl.multiple_of(j * rp, rp), rp)

    def mix_block(c, j):
        part = block_rows(j)
        return (0.5 * (0.7 * dv[c, part, :].astype(F32) - 0.3 * wv[c, part, :].astype(F32))).astype(BF16)

    for c in range(C):
        load(0, c).wait()
        load(1, c).wait()

        def send_block(k, _):
            d = distance(k)
            j = to(d)
            mixsrc[c, j] = mix_block(c, j)
            first_leg(c, d).start()
            return 0

        lax.fori_loop(1, reps, send_block, 0)
        owned[c][me] = mix_block(c, me)

    def turn_round(c):
        def arrived(d, _):
            first_leg_in(c, d).wait_recv()
            first_leg(c, d).wait_send()
            return 0

        lax.fori_loop(1, reps, arrived, 0)

        def send_back(k, _):
            d = distance(k)
            j = to(d)
            mixsrc[c, j] = owned[c][partner[j]]
            second_leg(c, d).start()
            return 0

        lax.fori_loop(1, reps, send_back, 0)
        mixin[c, me] = owned[c][partner[me]]

    def finish_momentum(c):
        load(2, c).wait()

        def arrived(d, _):
            second_leg_in(c, d).wait_recv()
            return 0

        lax.fori_loop(1, reps, arrived, 0)

        def block(j, _):
            part = block_rows(j)
            own = wv[c, part, :].astype(F32)
            moment = (0.5 * mv[c, part, :].astype(F32) + 0.35 * dv[c, part, :].astype(F32) + 0.15 * own
                      + mixin[c, j].astype(F32))
            mom_out[0, part, cols(c)] = moment.astype(BF16)
            base[0, part, cols(c)] = own - moment
            return 0

        lax.fori_loop(0, reps, block, 0)

    tile = 256

    def turn_tokens(s):
        def block(i, _):
            part = pl.ds(pl.multiple_of(i * tile, tile), tile)
            tokt[s, part, :] = tokv[s, :, part].T
            return 0

        lax.fori_loop(0, rows // tile, block, 0)

    def product(q, s, first):
        def block(i, _):
            part = pl.ds(pl.multiple_of(i * tile, tile), tile)
            term = jnp.dot(tokt[s, part, :], cotv[q, s], preferred_element_type=F32).astype(BF16).astype(F32)
            if first:
                grad[0, part, cols(q)] = term
            else:
                grad[0, part, cols(q)] += term
            return 0

        lax.fori_loop(0, rows // tile, block, 0)

    def add_squares(q):
        def block(i, _):
            g = grad[0, pl.ds(pl.multiple_of(i * 64, 64), 64), cols(q)]
            acc[...] += jnp.sum((g * g).reshape(8, 8, cw), axis=0)
            return 0

        lax.fori_loop(0, rows // 64, block, 0)

    def arrive(h, q):
        @pl.when(z - h >= 0)
        def _():
            s = lax.max(z - h, 0)
            right_copy(q, s, cotv.at[q, s]).wait_recv()

            @pl.when(z + 1 < n)
            def _():
                right_copy(q, s, cotv.at[q, s]).start()

        @pl.when(z + h < n)
        def _():
            s = lax.min(z + h, n - 1)
            left_copy(q, s, cotv.at[q, s]).wait_recv()

            @pl.when(z > 0)
            def _():
                left_copy(q, s, cotv.at[q, s]).start()

    def multiply(h, q):
        @pl.when(z - h >= 0)
        def _():
            s = lax.max(z - h, 0)
            if q == 0:
                tok_in(s, h).wait_recv()
                turn_tokens(s)
            product(q, s, False)

        @pl.when(z + h < n)
        def _():
            s = lax.min(z + h, n - 1)
            if q == 0:
                tok_in(s, n - h).wait_recv()
                turn_tokens(s)
            product(q, s, False)

        @pl.when(lax.max(z, n - 1 - z) == h)
        def _():
            add_squares(q)

    def tok_in(s, d):
        return pltpu.make_async_remote_copy(
            src_ref=tokv.at[s], dst_ref=tokv.at[s], send_sem=tsend.at[d], recv_sem=trecv.at[d],
            device_id=(me, s), device_id_type=MESH)

    acc[...] = jnp.zeros_like(acc)
    load_tok.wait()
    turn_tokens(z)
    for q in range(C):
        load_cot(q).wait()
        product(q, z, True)
    for h in range(1, n):
        for q in range(C):
            if h == n - 1 and q == C - 2:
                for c in range(C - 2):
                    finish_momentum(c)
            if h == n - 1 and q == C - 1:
                finish_momentum(C - 2)
            arrive(h, q)
            if h == 1:
                turn_round(q)
            if h > 1:
                multiply(h - 1, q)
            if h == n - 1:
                multiply(h, q)

    part_sum = acc[:, 0:128]
    for k in range(1, cw // 128):
        part_sum = part_sum + acc[:, k * 128 : (k + 1) * 128]
    squares[z] = part_sum

    def squares_copy(d):
        k = lax.rem(z + d, n)
        return pltpu.make_async_remote_copy(
            src_ref=squares.at[z], dst_ref=squares.at[z], send_sem=qsend.at[d], recv_sem=qrecv.at[d],
            device_id=(me, k), device_id_type=MESH)

    for d in range(1, n):
        squares_copy(d).start()
    finish_momentum(C - 1)
    for d in range(1, n):
        s = lax.rem(z + n - d, n)
        pltpu.make_async_remote_copy(
            src_ref=squares.at[s], dst_ref=squares.at[s], send_sem=qsend.at[d], recv_sem=qrecv.at[d],
            device_id=(me, s), device_id_type=MESH).wait_recv()
    total = jnp.sum(jnp.sum(squares[...], axis=0), axis=(0, 1), keepdims=True)
    factor = 0.5 / jnp.sqrt(total / (rows * n * C * cw) + 1e-06)
    factor_out[...] = jnp.broadcast_to(factor[None], factor_out.shape)

    for d in range(1, n):
        tok_copy(d).wait_send()
        squares_copy(d).wait_send()
    for q in range(C):
        for h in range(0, n):
            @pl.when((z - h >= 0) & (z + 1 < n))
            def _():
                s = lax.max(z - h, 0)
                right_copy(q, s, cotv.at[q, s]).wait_send()

            @pl.when((z + h < n) & (z > 0))
            def _():
                s = lax.min(z + h, n - 1)
                left_copy(q, s, cotv.at[q, s]).wait_send()

        def sent(d, _):
            second_leg(q, d).wait_send()
            return 0

        lax.fori_loop(1, reps, sent, 0)


def last_pass(parts, moment, base, grad, factor, mom_out, w_out, held, sem):
    depth = held.shape[1]
    step = 16
    mom_copy = pltpu.make_async_copy(moment, mom_out, sem.at[parts])
    mom_copy.start()
    copies = []
    for k in range(parts):
        def block(i, _):
            part = pl.ds(pl.multiple_of(k * depth + i * step, step), step)
            held[k, pl.ds(pl.multiple_of(i * step, step), step), :] = (
                base[0, part, :] - grad[0, part, :] * factor[0]
            ).astype(BF16)
            return 0

        lax.fori_loop(0, depth // step, block, 0)
        copies.append(pltpu.make_async_copy(held.at[k], w_out.at[0, pl.ds(k * depth, depth), :], sem.at[k]))
        copies[-1].start()
    for copy in copies:
        copy.wait()
    mom_copy.wait()


def on_device(reps, n, tokens, cotangent, w_slow, drift, momentum, partner):
    C = CHUNKS
    _, toks, d_in = tokens.shape
    _, rows, d_out = w_slow.shape
    cw, rp, cd = d_out // C, rows // reps, d_in // n
    hbm = pl.BlockSpec(memory_space=pl.ANY)
    dma = pltpu.SemaphoreType.DMA
    scratch = [
        pltpu.VMEM((C, rows, cw), BF16),
        pltpu.VMEM((C, rows, cw), BF16),
        pltpu.VMEM((C, rows, cw), BF16),
        pltpu.VMEM((n, toks, cd), BF16),
        pltpu.VMEM((C, n, toks, cw), BF16),
        pltpu.VMEM((C, reps, rp, cw), BF16),
        pltpu.VMEM((C, reps, rp, cw), BF16),
        pltpu.VMEM((n, 8, 128), F32),
        pltpu.VMEM((8, cw), F32),
        pltpu.VMEM((n, cd, toks), BF16),
    ]
    scratch += [pltpu.VMEM((reps, rp, cw), BF16) for _ in range(C)]
    scratch += [
        dma((5, C)), dma((n,)), dma((n,)), dma((C, n)), dma((C, n)), dma((C, n)),
        dma((C, reps)), dma((C, reps)), dma((C, reps)), dma((C, reps)), dma((n,)), dma((n,)),
    ]
    moment, base, grad, factor = pl.pallas_call(
        functools.partial(kernel, reps, n),
        out_shape=(
            pltpu.VMEM(momentum.shape, BF16),
            pltpu.VMEM(w_slow.shape, F32),
            pltpu.VMEM(w_slow.shape, F32),
            pltpu.VMEM((1, 1, d_out), F32),
        ),
        in_specs=[hbm] * 5 + [pl.BlockSpec(memory_space=pltpu.SMEM)],
        out_specs=[pl.BlockSpec(memory_space=pltpu.VMEM)] * 4,
        scratch_shapes=scratch,
        compiler_params=pltpu.CompilerParams(
            collective_id=0, has_side_effects=True, vmem_limit_bytes=34 * 1024 * 1024
        ),
        cost_estimate=pl.CostEstimate(
            flops=2 * n * toks * rows * d_out, bytes_accessed=5 * rows * d_out * 2, transcendentals=0
        ),
    )(tokens, cotangent, w_slow, drift, momentum, partner)
    parts = 8
    return pl.pallas_call(
        functools.partial(last_pass, parts),
        out_shape=(jax.ShapeDtypeStruct(momentum.shape, BF16), jax.ShapeDtypeStruct(w_slow.shape, BF16)),
        in_specs=[pl.BlockSpec(memory_space=pltpu.VMEM)] * 4,
        out_specs=(hbm, hbm),
        scratch_shapes=[pltpu.VMEM((parts, rows // parts, d_out), BF16), dma((parts + 1,))],
        compiler_params=pltpu.CompilerParams(vmem_limit_bytes=8 * 1024 * 1024),
        cost_estimate=pl.CostEstimate(flops=2 * rows * d_out, bytes_accessed=4 * rows * d_out, transcendentals=0),
    )(moment, base, grad, factor)


def solution(mesh):
    spec = P("rep", "fsdp", None)
    return jax.shard_map(
        functools.partial(on_device, mesh.shape["rep"], mesh.shape["fsdp"]),
        mesh=mesh,
        in_specs=(spec, spec, spec, spec, spec, P()),
        out_specs=(spec, spec),
        check_vma=False,
    )
```

```python
import functools

import jax
import jax.numpy as jnp
from jax import lax
from jax.experimental import pallas as pl
from jax.experimental.pallas import tpu as pltpu
from jax.sharding import PartitionSpec as P

MESH = pl.DeviceIdType.MESH
CHUNKS = 2
F32 = jnp.float32
BF16 = jnp.bfloat16


def kernel(reps, n, *refs):
    C = CHUNKS
    (tok, cot, slow, drift, mom, partner, mom_out, base, grad, factor_out) = refs[:10]
    (wv, dv, mv, tokv, cotv, mixsrc, mixin, squares, acc, tokt) = refs[10:20]
    owned = refs[20 : 20 + C]
    (ld, tsend, trecv, crecv, crsend, clsend, asend, arecv, bsend, brecv, qsend, qrecv) = refs[20 + C :]
    me = lax.axis_index("rep")
    z = lax.axis_index("fsdp")
    rows = wv.shape[1]
    cw = wv.shape[2]
    rp = rows // reps
    cd = tokv.shape[2]

    bits = reps.bit_length() - 1
    paired = reps == 1 << bits

    def bit(value, i):
        return lax.rem(lax.div(value, 1 << i), 2)

    def to(d):
        if not paired:
            return lax.rem(me + d, reps)
        return sum((bit(me, i) + bit(d, i) - 2 * bit(me, i) * bit(d, i)) * (1 << i) for i in range(bits))

    def source(d):
        return to(d) if paired else lax.rem(me + reps - d, reps)

    def distance(k):
        if not paired or bits < 3:
            return k
        d = lax.rem(k, reps - 1) + 1
        return d + 2 * (bit(d, 1) - bit(d, 2)) * lax.rem(me, 2)

    def cols(c):
        return pl.ds(c * cw, cw)

    def load(kind, c):
        src, dst = ((slow, wv), (drift, dv), (mom, mv))[kind]
        return pltpu.make_async_copy(src.at[0, :, cols(c)], dst.at[c], ld.at[kind, c])

    def load_cot(q):
        return pltpu.make_async_copy(cot.at[0, :, cols(q)], cotv.at[q, z], ld.at[3, q])

    def tok_cols(k):
        return pl.ds(pl.multiple_of(k * cd, 128), cd)

    load_tok = pltpu.make_async_copy(tok.at[0, :, tok_cols(z)], tokv.at[z], ld.at[4, 0])

    for c in range(C):
        load(0, c).start()
        load(1, c).start()

    barrier = pltpu.get_barrier_semaphore()
    for d in range(1, n):
        pl.semaphore_signal(barrier, inc=1, device_id=(me, lax.rem(z + d, n)), device_id_type=MESH)

    def greet(d, _):
        pl.semaphore_signal(barrier, inc=1, device_id=(lax.rem(me + d, reps), z), device_id_type=MESH)
        return 0

    lax.fori_loop(1, reps, greet, 0)
    for q in range(C):
        load_cot(q).start()
    load_tok.start()
    for c in range(C):
        load(2, c).start()
    pl.semaphore_wait(barrier, reps - 1 + n - 1)

    def right_copy(q, s, src):
        return pltpu.make_async_remote_copy(
            src_ref=src, dst_ref=cotv.at[q, s], send_sem=crsend.at[q, s], recv_sem=crecv.at[q, s],
            device_id=(me, lax.min(z + 1, n - 1)), device_id_type=MESH)

    def left_copy(q, s, src):
        return pltpu.make_async_remote_copy(
            src_ref=src, dst_ref=cotv.at[q, s], send_sem=clsend.at[q, s], recv_sem=crecv.at[q, s],
            device_id=(me, lax.max(z - 1, 0)), device_id_type=MESH)

    for q in range(C):
        @pl.when(z + 1 < n)
        def _():
            right_copy(q, z, cot.at[0, :, cols(q)]).start()

        @pl.when(z > 0)
        def _():
            left_copy(q, z, cot.at[0, :, cols(q)]).start()

    def tok_copy(d):
        k = lax.rem(z + d, n)
        return pltpu.make_async_remote_copy(
            src_ref=tok.at[0, :, tok_cols(k)], dst_ref=tokv.at[z], send_sem=tsend.at[d], recv_sem=trecv.at[d],
            device_id=(me, k), device_id_type=MESH)

    for d in range(1, n):
        tok_copy(d).start()

    def first_leg(c, d):
        j = to(d)
        return pltpu.make_async_remote_copy(
            src_ref=mixsrc.at[c, j], dst_ref=owned[c].at[me], send_sem=asend.at[c, d], recv_sem=arecv.at[c, d],
            device_id=(j, z), device_id_type=MESH)

    def first_leg_in(c, d):
        s = source(d)
        return pltpu.make_async_remote_copy(
            src_ref=mixsrc.at[c, s], dst_ref=owned[c].at[s], send_sem=asend.at[c, d], recv_sem=arecv.at[c, d],
            device_id=(s, z), device_id_type=MESH)

    def second_leg(c, d):
        j = to(d)
        return pltpu.make_async_remote_copy(
            src_ref=mixsrc.at[c, j], dst_ref=mixin.at[c, me], send_sem=bsend.at[c, d], recv_sem=brecv.at[c, d],
            device_id=(j, z), device_id_type=MESH)

    def second_leg_in(c, d):
        s = source(d)
        return pltpu.make_async_remote_copy(
            src_ref=mixsrc.at[c, s], dst_ref=mixin.at[c, s], send_sem=bsend.at[c, d], recv_sem=brecv.at[c, d],
            device_id=(s, z), device_id_type=MESH)

    def block_rows(j):
        return pl.ds(pl.multiple_of(j * rp, rp), rp)

    def mix_block(c, j):
        part = block_rows(j)
        return (0.5 * (0.7 * dv[c, part, :].astype(F32) - 0.3 * wv[c, part, :].astype(F32))).astype(BF16)

    for c in range(C):
        load(0, c).wait()
        load(1, c).wait()

        def send_block(k, _):
            d = distance(k)
            j = to(d)
            mixsrc[c, j] = mix_block(c, j)
            first_leg(c, d).start()
            return 0

        lax.fori_loop(1, reps, send_block, 0)
        owned[c][me] = mix_block(c, me)

    def turn_round(c):
        def arrived(d, _):
            first_leg_in(c, d).wait_recv()
            first_leg(c, d).wait_send()
            return 0

        lax.fori_loop(1, reps, arrived, 0)

        def send_back(k, _):
            d = distance(k)
            j = to(d)
            mixsrc[c, j] = owned[c][partner[j]]
            second_leg(c, d).start()
            return 0

        lax.fori_loop(1, reps, send_back, 0)
        mixin[c, me] = owned[c][partner[me]]

    def finish_momentum(c):
        load(2, c).wait()

        def arrived(d, _):
            second_leg_in(c, d).wait_recv()
            return 0

        lax.fori_loop(1, reps, arrived, 0)

        def block(j, _):
            part = block_rows(j)
            own = wv[c, part, :].astype(F32)
            moment = (0.5 * mv[c, part, :].astype(F32) + 0.35 * dv[c, part, :].astype(F32) + 0.15 * own
                      + mixin[c, j].astype(F32))
            mom_out[0, part, cols(c)] = moment.astype(BF16)
            base[0, part, cols(c)] = own - moment
            return 0

        lax.fori_loop(0, reps, block, 0)

    tile = 256

    def turn_tokens(s):
        def block(i, _):
            part = pl.ds(pl.multiple_of(i * tile, tile), tile)
            tokt[s, part, :] = tokv[s, :, part].T
            return 0

        lax.fori_loop(0, rows // tile, block, 0)

    def product(q, s, first):
        def block(i, _):
            part = pl.ds(pl.multiple_of(i * tile, tile), tile)
            term = jnp.dot(tokt[s, part, :], cotv[q, s], preferred_element_type=F32).astype(BF16).astype(F32)
            if first:
                grad[0, part, cols(q)] = term
            else:
                grad[0, part, cols(q)] += term
            return 0

        lax.fori_loop(0, rows // tile, block, 0)

    def add_squares(q):
        def block(i, _):
            g = grad[0, pl.ds(pl.multiple_of(i * 64, 64), 64), cols(q)]
            acc[...] += jnp.sum((g * g).reshape(8, 8, cw), axis=0)
            return 0

        lax.fori_loop(0, rows // 64, block, 0)

    def arrive(h, q):
        @pl.when(z - h >= 0)
        def _():
            s = lax.max(z - h, 0)
            right_copy(q, s, cotv.at[q, s]).wait_recv()

            @pl.when(z + 1 < n)
            def _():
                right_copy(q, s, cotv.at[q, s]).start()

        @pl.when(z + h < n)
        def _():
            s = lax.min(z + h, n - 1)
            left_copy(q, s, cotv.at[q, s]).wait_recv()

            @pl.when(z > 0)
            def _():
                left_copy(q, s, cotv.at[q, s]).start()

    def multiply(h, q):
        @pl.when(z - h >= 0)
        def _():
            s = lax.max(z - h, 0)
            if q == 0:
                tok_in(s, h).wait_recv()
                turn_tokens(s)
            product(q, s, False)

        @pl.when(z + h < n)
        def _():
            s = lax.min(z + h, n - 1)
            if q == 0:
                tok_in(s, n - h).wait_recv()
                turn_tokens(s)
            product(q, s, False)

        @pl.when(lax.max(z, n - 1 - z) == h)
        def _():
            add_squares(q)

    def tok_in(s, d):
        return pltpu.make_async_remote_copy(
            src_ref=tokv.at[s], dst_ref=tokv.at[s], send_sem=tsend.at[d], recv_sem=trecv.at[d],
            device_id=(me, s), device_id_type=MESH)

    acc[...] = jnp.zeros_like(acc)
    load_tok.wait()
    turn_tokens(z)
    for q in range(C):
        load_cot(q).wait()
        product(q, z, True)
    for h in range(1, n):
        for q in range(C):
            if h == n - 1 and q == C - 2:
                for c in range(C - 2):
                    finish_momentum(c)
            if h == n - 1 and q == C - 1:
                finish_momentum(C - 2)
            arrive(h, q)
            if h == 1:
                turn_round(q)
            if h > 1:
                multiply(h - 1, q)
            if h == n - 1:
                multiply(h, q)

    part_sum = acc[:, 0:128]
    for k in range(1, cw // 128):
        part_sum = part_sum + acc[:, k * 128 : (k + 1) * 128]
    squares[z] = part_sum

    def squares_copy(d):
        k = lax.rem(z + d, n)
        return pltpu.make_async_remote_copy(
            src_ref=squares.at[z], dst_ref=squares.at[z], send_sem=qsend.at[d], recv_sem=qrecv.at[d],
            device_id=(me, k), device_id_type=MESH)

    for d in range(1, n):
        squares_copy(d).start()
    finish_momentum(C - 1)
    for d in range(1, n):
        s = lax.rem(z + n - d, n)
        pltpu.make_async_remote_copy(
            src_ref=squares.at[s], dst_ref=squares.at[s], send_sem=qsend.at[d], recv_sem=qrecv.at[d],
            device_id=(me, s), device_id_type=MESH).wait_recv()
    total = jnp.sum(jnp.sum(squares[...], axis=0), axis=(0, 1), keepdims=True)
    factor = 0.5 / jnp.sqrt(total / (rows * n * C * cw) + 1e-06)
    factor_out[...] = jnp.broadcast_to(factor[None], factor_out.shape)

    for d in range(1, n):
        tok_copy(d).wait_send()
        squares_copy(d).wait_send()
    for q in range(C):
        for h in range(0, n):
            @pl.when((z - h >= 0) & (z + 1 < n))
            def _():
                s = lax.max(z - h, 0)
                right_copy(q, s, cotv.at[q, s]).wait_send()

            @pl.when((z + h < n) & (z > 0))
            def _():
                s = lax.min(z + h, n - 1)
                left_copy(q, s, cotv.at[q, s]).wait_send()

        def sent(d, _):
            second_leg(q, d).wait_send()
            return 0

        lax.fori_loop(1, reps, sent, 0)


def last_pass(parts, moment, base, grad, factor, mom_out, w_out, held, sem):
    depth = held.shape[1]
    step = 16
    mom_copy = pltpu.make_async_copy(moment, mom_out, sem.at[parts])
    mom_copy.start()
    copies = []
    for k in range(parts):
        def block(i, _):
            part = pl.ds(pl.multiple_of(k * depth + i * step, step), step)
            held[k, pl.ds(pl.multiple_of(i * step, step), step), :] = (
                base[0, part, :] - grad[0, part, :] * factor[0]
            ).astype(BF16)
            return 0

        lax.fori_loop(0, depth // step, block, 0)
        copies.append(pltpu.make_async_copy(held.at[k], w_out.at[0, pl.ds(k * depth, depth), :], sem.at[k]))
        copies[-1].start()
    for copy in copies:
        copy.wait()
    mom_copy.wait()


def on_device(reps, n, tokens, cotangent, w_slow, drift, momentum, partner):
    C = CHUNKS
    _, toks, d_in = tokens.shape
    _, rows, d_out = w_slow.shape
    cw, rp, cd = d_out // C, rows // reps, d_in // n
    hbm = pl.BlockSpec(memory_space=pl.ANY)
    dma = pltpu.SemaphoreType.DMA
    scratch = [
        pltpu.VMEM((C, rows, cw), BF16),
        pltpu.VMEM((C, rows, cw), BF16),
        pltpu.VMEM((C, rows, cw), BF16),
        pltpu.VMEM((n, toks, cd), BF16),
        pltpu.VMEM((C, n, toks, cw), BF16),
        pltpu.VMEM((C, reps, rp, cw), BF16),
        pltpu.VMEM((C, reps, rp, cw), BF16),
        pltpu.VMEM((n, 8, 128), F32),
        pltpu.VMEM((8, cw), F32),
        pltpu.VMEM((n, cd, toks), BF16),
    ]
    scratch += [pltpu.VMEM((reps, rp, cw), BF16) for _ in range(C)]
    scratch += [
        dma((5, C)), dma((n,)), dma((n,)), dma((C, n)), dma((C, n)), dma((C, n)),
        dma((C, reps)), dma((C, reps)), dma((C, reps)), dma((C, reps)), dma((n,)), dma((n,)),
    ]
    moment, base, grad, factor = pl.pallas_call(
        functools.partial(kernel, reps, n),
        out_shape=(
            pltpu.VMEM(momentum.shape, BF16),
            pltpu.VMEM(w_slow.shape, F32),
            pltpu.VMEM(w_slow.shape, F32),
            pltpu.VMEM((1, 1, d_out), F32),
        ),
        in_specs=[hbm] * 5 + [pl.BlockSpec(memory_space=pltpu.SMEM)],
        out_specs=[pl.BlockSpec(memory_space=pltpu.VMEM)] * 4,
        scratch_shapes=scratch,
        compiler_params=pltpu.CompilerParams(
            collective_id=0, has_side_effects=True, vmem_limit_bytes=34 * 1024 * 1024
        ),
        cost_estimate=pl.CostEstimate(
            flops=2 * n * toks * rows * d_out, bytes_accessed=5 * rows * d_out * 2, transcendentals=0
        ),
    )(tokens, cotangent, w_slow, drift, momentum, partner)
    parts = 8
    return pl.pallas_call(
        functools.partial(last_pass, parts),
        out_shape=(jax.ShapeDtypeStruct(momentum.shape, BF16), jax.ShapeDtypeStruct(w_slow.shape, BF16)),
        in_specs=[pl.BlockSpec(memory_space=pltpu.VMEM)] * 4,
        out_specs=(hbm, hbm),
        scratch_shapes=[pltpu.VMEM((parts, rows // parts, d_out), BF16), dma((parts + 1,))],
        compiler_params=pltpu.CompilerParams(vmem_limit_bytes=8 * 1024 * 1024),
        cost_estimate=pl.CostEstimate(flops=2 * rows * d_out, bytes_accessed=4 * rows * d_out, transcendentals=0),
    )(moment, base, grad, factor)


def solution(mesh):
    spec = P("rep", "fsdp", None)
    return jax.shard_map(
        functools.partial(on_device, mesh.shape["rep"], mesh.shape["fsdp"]),
        mesh=mesh,
        in_specs=(spec, spec, spec, spec, spec, P()),
        out_specs=(spec, spec),
        check_vma=False,
    )
```
